512 devices in a mesh: mic: 64 (over z, x), src: 8 (over y, core).
Axes of the slice: x: 4, y: 4, z: 16, core: 2. Of those that a mesh axis runs over, the one named last changes fastest.
Arguments:
- tensor_slab: bfloat16 [32, 4096, 8192], P(None, 'src', 'mic'), may hold values from -6 to 6
- observed_blocks: int32 [64, 64], P('src', 'mic'), may hold values 0 or 1
- mic_factor: float32 [8192, 256], P('mic'), may hold values from -40 to 40
- time_factor: float32 [32, 256], replicated, may hold values from -6 to 6
Outputs:
- source_out: float32 [4096, 256], P('src')
- mic_out: float32 [8192, 256], P('mic')
- time_out: float32 [32, 256], replicated
The draws below stay inside these ranges and needn't reach their ends.
All inputs are finite; a program needn't handle non-finite values. No bound on the sum of `observed_blocks` on one device may be relied on, other than what follows from the above.
Results may differ from the reference program's by a relative error of at most 0.012.
Values sent between devices are 32-bit elements; how exact they have to be, the bound alone decides.
A program may use at most 64 MiB of HBM per device.

```python
import jax
import jax.numpy as jnp
from jax import lax

R = 256
K = 32
MIC_DEV = 128
SRC_BLK = 64
MIC_BLK = 128
S = 4096
M = 8192


def draw_mic_factor(key, part):
    key = jax.random.fold_in(key, 11)
    key_vals, key_rows = jax.random.split(key)
    values = jnp.clip(jax.random.normal(key_vals, (M, R), jnp.float32), -4.0, 4.0)
    row_noise = jnp.exp(jax.random.uniform(key_rows, (M, 1), jnp.float32, 0.0, 0.693))
    position = jnp.arange(M, dtype=jnp.float32)[:, None]
    center = M // 2 + MIC_DEV // 2
    offset = (position - center) / MIC_DEV
    bump = jnp.exp(-offset * offset)
    return values * row_noise * (1.0 + 4.0 * bump)


def plant(entries, own_key, least, largest):
    extent = entries.shape
    place = [jax.random.randint(jax.random.fold_in(own_key, axis), (), 0, extent[axis]) for axis in range(len(extent))]
    entries = entries.at[tuple(place)].set(least)
    longest = extent.index(max(extent))
    place[longest] = (place[longest] + 1) % extent[longest]
    return entries.at[tuple(place)].set(largest)


def shard_levels(rng, dims, pieces, low, largest):
    level = 1.0
    for dim, shards_of in pieces:
        heights = jax.random.uniform(jax.random.fold_in(jax.random.fold_in(rng, 6), dim), (shards_of,), jnp.float32, low / len(pieces), largest / len(pieces))
        level = level * jnp.repeat(jnp.exp(heights), dims[dim] // shards_of).reshape((-1,) + (1,) * (len(dims) - 1 - dim))
    return level


def bell_draw(rng, extent, scale, bound, cuts=(), kind=jnp.bfloat16):
    result = jax.random.normal(rng, extent, jnp.float32) * scale
    if len(cuts) > 0:
        result = shard_levels(rng, extent, cuts, -0.22, 0.18) * result
    return jnp.clip(result, min=-bound, max=bound).astype(kind)


def setup_inputs(seed: int = 0) -> dict:
    streams_of = jax.random.split(jax.random.key(seed), 5)
    return {
        "tensor_slab": bell_draw(streams_of[0], (K, S, M), 1.0, 6.0, ((1, 8), (2, 64))),
        "observed_blocks": plant((jax.random.randint(streams_of[1], (S // SRC_BLK, M // MIC_BLK), 0, 4) < 3).astype(jnp.int32), jax.random.fold_in(streams_of[1], 1), 0, 1),
        "mic_factor": draw_mic_factor(jax.random.fold_in(streams_of[4], 71), 0),
        "time_factor": bell_draw(streams_of[3], (K, R), 1.0, 6.0, (), jnp.float32),
    }


def expand_blocks(blocks):
    rows_blocks, cols_blocks = blocks.shape
    spread = jnp.broadcast_to(blocks[:, None, :, None], (rows_blocks, SRC_BLK, cols_blocks, MIC_BLK))
    return spread.reshape(rows_blocks * SRC_BLK, cols_blocks * MIC_BLK).astype(jnp.bfloat16)

def gram_of(factor):
    return jnp.dot(factor.T.astype(jnp.float32), factor.astype(jnp.float32), precision=lax.Precision.HIGHEST, preferred_element_type=jnp.float32)

def normalize(raw, gram, count):
    scales = jnp.sqrt(jnp.diagonal(gram) / count + 1e-06)
    return (raw / scales[None, :], gram / (scales[:, None] * scales[None, :]))

def solve_rows(system, right):
    lower = jnp.linalg.cholesky(system)
    middle = lax.linalg.triangular_solve(lower, right, left_side=False, lower=True, transpose_a=True)
    return lax.linalg.triangular_solve(lower, middle, left_side=False, lower=True, transpose_a=False)

def reference(tensor_slab, observed_blocks, mic_factor, time_factor):
    keep = expand_blocks(observed_blocks)
    samples, src_total, mic_total = tensor_slab.shape
    rank = mic_factor.shape[1]
    gram_time = gram_of(time_factor)
    mic_low = mic_factor.astype(jnp.bfloat16)

    def source_step(total, pair):
        slab, weight = pair
        piece = slab * keep
        khatri = (weight[None, :] * mic_low.astype(jnp.float32)).astype(jnp.bfloat16)
        return (total + jnp.dot(piece.astype(jnp.float32), khatri.astype(jnp.float32), preferred_element_type=jnp.float32), None)
    source_mttkrp, _ = lax.scan(source_step, jnp.zeros((src_total, rank), jnp.float32), (tensor_slab, time_factor))
    system_src = gram_of(mic_factor) * gram_time / (mic_total * samples)
    source_raw = solve_rows(system_src, source_mttkrp)
    source_out, gram_src = normalize(source_raw, gram_of(source_raw), src_total)
    src_low = source_out.astype(jnp.bfloat16)

    def mic_step(total, pair):
        slab, weight = pair
        piece = slab * keep
        khatri = (weight[None, :] * src_low.astype(jnp.float32)).astype(jnp.bfloat16)
        return (total + jnp.dot(piece.T.astype(jnp.float32), khatri.astype(jnp.float32), preferred_element_type=jnp.float32), None)
    mic_mttkrp, _ = lax.scan(mic_step, jnp.zeros((mic_total, rank), jnp.float32), (tensor_slab, time_factor))
    system_mic = gram_src * gram_time / (src_total * samples)
    mic_raw = solve_rows(system_mic, mic_mttkrp)
    mic_out, gram_mic = normalize(mic_raw, gram_of(mic_raw), mic_total)
    mic_new_low = mic_out.astype(jnp.bfloat16)

    def time_step(carry, slab):
        piece = slab * keep
        inner = jnp.dot(piece.astype(jnp.float32), mic_new_low.astype(jnp.float32), preferred_element_type=jnp.float32)
        return (carry, lax.optimization_barrier(jnp.sum(inner * source_out, axis=0)))
    _, time_mttkrp = lax.scan(time_step, jnp.float32(0.0), tensor_slab)
    system_time = gram_src * gram_mic / (src_total * mic_total)
    time_raw = solve_rows(system_time, time_mttkrp)
    time_out, _ = normalize(time_raw, gram_of(time_raw), samples)
    return (source_out, mic_out, time_out)
```

```python
import functools

import jax
import jax.numpy as jnp
from jax import lax
from jax.experimental import pallas as pl
from jax.experimental.pallas import tpu as pltpu
from jax.sharding import PartitionSpec as P

MESH = pl.DeviceIdType.MESH
F32 = jnp.float32
BF16 = jnp.bfloat16

RANK = 256
SAMPLES = 32
SRC_DEV = 512
MIC_DEV = 128
SRC_BLK = 64
NX = 4
NZ = 16
NSRC = 8
NXS = NX * NSRC
SRC_ALL = SRC_DEV * NSRC
MIC_ALL = MIC_DEV * NX * NZ
BLK = 32


def exact_dot(a, b, dims=((1,), (0,))):
    return lax.dot_general(
        a, b, (dims, ((), ())), precision=lax.Precision.HIGHEST, preferred_element_type=F32
    )


def split3(a):
    first = a.astype(BF16)
    rest = a - first.astype(F32)
    second = rest.astype(BF16)
    third = (rest - second.astype(F32)).astype(BF16)
    return first, second, third


def outer_dot(a, b):
    a0, a1, a2 = split3(a)
    b0, b1, b2 = split3(b)
    left = jnp.concatenate([a0, a0, a1, a1, a0, a2], axis=0)
    right = jnp.concatenate([b0, b1, b0, b1, b2, b0], axis=0)
    return lax.dot_general(left, right, (((0,), (0,)), ((), ())), preferred_element_type=F32)


def invert(a_ref):
    lane = lax.broadcasted_iota(jnp.int32, (BLK, RANK), 1)
    sub = lax.broadcasted_iota(jnp.int32, (BLK, RANK), 0)
    lane_row = lax.broadcasted_iota(jnp.int32, (1, RANK), 1)

    def block(i, carry):
        base = pl.multiple_of(i * BLK, BLK)
        old = a_ref[pl.ds(base, BLK), :]
        panel = pltpu.roll(old, RANK - base, 1)
        for j in range(BLK):
            column = panel[:, j : j + 1]
            inv = 1.0 / panel[j : j + 1, j : j + 1]
            row = jnp.where(lane_row == j, inv, panel[j : j + 1, :] * inv)
            other = jnp.where(lane == j, 0.0, panel) - column * row
            panel = jnp.where(sub == j, row, other)
        panel = pltpu.roll(panel, base, 1)
        inside = (lane_row >= base) & (lane_row < base + BLK)
        column = jnp.where(lane < base, -old, old)
        update = outer_dot(column, panel)
        a_ref[...] = jnp.where(inside, 0.0, a_ref[...]) - update
        a_ref[pl.ds(base, BLK), :] = panel
        return carry

    lax.fori_loop(0, RANK // BLK, block, 0)


def diagonal(gram):
    rows = lax.broadcasted_iota(jnp.int32, (RANK, RANK), 0)
    cols = lax.broadcasted_iota(jnp.int32, (RANK, RANK), 1)
    only = jnp.where(rows == cols, gram, 0.0)
    return jnp.sum(only, axis=0, keepdims=True), jnp.sum(only, axis=1, keepdims=True)


def scales_of(gram, count):
    row, col = diagonal(gram)
    return jnp.sqrt(row / count + 1e-06), jnp.sqrt(col / count + 1e-06)


def drain(ref, sem):
    pltpu.make_async_copy(ref, ref, sem).wait()


def kernel(
    x_hbm,
    blk_ref,
    mic_ref,
    time_ref,
    src_out,
    mic_out,
    time_out,
    x_v,
    xt_v,
    kr_v,
    p_v,
    y_v,
    yx_v,
    y128_v,
    yz_v,
    raw8_v,
    raw_v,
    low_v,
    gram_v,
    g2_v,
    g3_v,
    gn_v,
    gx_v,
    gz_v,
    g8_v,
    gram1_v,
    a_v,
    gt_v,
    gs_v,
    gs8_v,
    gram2_v,
    mm_v,
    mr_v,
    mraw_v,
    t_v,
    tr_v,
    hx_v,
    h_v,
    hz_v,
    h2_v,
    hy_v,
    h3_v,
    gram3_v,
    load_sem,
    send_sem,
    recv_sem,
):
    me_mic = lax.axis_index("mic")
    src = lax.axis_index("src")
    z = me_mic // NX
    x = me_mic % NX
    p = x * NSRC + src

    def at(zz, xx, ss):
        return (zz * NX + xx, ss)

    load = pltpu.make_async_copy(x_hbm, x_v, load_sem)
    load.start()

    barrier = pltpu.get_barrier_semaphore()

    def greet_z(d, c):
        pl.semaphore_signal(barrier, inc=1, device_id=at((z + d) % NZ, x, src), device_id_type=MESH)
        return c

    def greet_xs(d, c):
        q = (p + d) % NXS
        pl.semaphore_signal(
            barrier, inc=1, device_id=at(z, q // NSRC, q % NSRC), device_id_type=MESH
        )
        return c

    lax.fori_loop(1, NZ, greet_z, 0)
    lax.fori_loop(1, NXS, greet_xs, 0)

    def send(src_ref, dst_ref, stage, device):
        pltpu.make_async_remote_copy(
            src_ref=src_ref,
            dst_ref=dst_ref,
            send_sem=send_sem.at[stage],
            recv_sem=recv_sem.at[stage],
            device_id=device,
            device_id_type=MESH,
        ).start()

    def gather_xs(piece_ref, full_ref, stage):
        def one(d, c):
            q = (p + d) % NXS
            send(piece_ref, full_ref.at[p], stage, at(z, q // NSRC, q % NSRC))
            return c

        lax.fori_loop(1, NXS, one, 0)

    mic = mic_ref[...]
    gram_v[...] = exact_dot(mic, mic, ((0,), (0,)))
    times = time_ref[...]
    gt_v[...] = exact_dot(times, times, ((0,), (0,)))
    mic_low = mic.astype(BF16).astype(F32)

    def make_kr(k, c):
        kr_v[pl.ds(pl.multiple_of(k * MIC_DEV, MIC_DEV), MIC_DEV), :] = (
            time_ref[pl.ds(k, 1), :] * mic_low
        ).astype(BF16)
        return c

    lax.fori_loop(0, SAMPLES, make_kr, 0)

    pl.semaphore_wait(barrier, NZ - 1 + NXS - 1)

    def gram_x(gram_ref, dst, stage):
        def one(d, c):
            xx = (x + d) % NX
            rows = pl.ds(pl.multiple_of(xx * 64 + src * 8, 8), 8)
            send(gram_ref.at[rows, :], dst.at[x], stage, at(z, xx, src))
            return c

        lax.fori_loop(1, NX, one, 0)

    own_rows = pl.ds(pl.multiple_of(x * 64 + src * 8, 8), 8)
    gram_x(gram_v, gx_v, 0)
    gx_v[x] = gram_v[own_rows, :]

    load.wait()

    def chunk(d, c):
        xx = (x + d) % NX
        start = xx * 128

        def part(kk, acc):
            left = jnp.concatenate(
                [x_v[kk * 8 + i, pl.ds(pl.multiple_of(start, 128), 128), :] for i in range(8)],
                axis=1,
            )
            right = kr_v[pl.ds(pl.multiple_of(kk * 1024, 1024), 1024), :]
            return acc + jnp.dot(left, right, preferred_element_type=F32)

        acc = lax.fori_loop(0, SAMPLES // 8, part, jnp.zeros((128, RANK), F32))
        for h in range(2):
            keep = blk_ref[xx * 2 + h, 0].astype(F32)
            y_v[pl.ds(pl.multiple_of(start + h * 64, 64), 64), :] = (
                acc[h * 64 : (h + 1) * 64, :] * keep
            )
        return c

    def chunk_send(d, c):
        chunk(d, c)
        xx = (x + d) % NX
        rows = pl.ds(pl.multiple_of(xx * 128, 128), 128)
        send(y_v.at[rows, :], yx_v.at[x], 1, at(z, xx, src))
        return c

    lax.fori_loop(1, NX, chunk_send, 0)
    chunk(0, 0)

    drain(gx_v.at[pl.ds(0, NX - 1)], recv_sem.at[0])
    g8_v[...] = (gx_v[0] + gx_v[1]) + (gx_v[2] + gx_v[3])

    def gram_z(d, c):
        zz = (z + d) % NZ
        send(g8_v, gz_v.at[z], 2, at(zz, x, src))
        return c

    lax.fori_loop(1, NZ, gram_z, 0)
    gz_v[z] = g8_v[...]

    yx_v[x] = y_v[pl.ds(pl.multiple_of(x * 128, 128), 128), :]
    drain(yx_v.at[pl.ds(0, NX - 1)], recv_sem.at[1])
    y128_v[...] = (yx_v[0] + yx_v[1]) + (yx_v[2] + yx_v[3])

    def rows_z(d, c):
        zz = (z + d) % NZ
        send(y128_v.at[pl.ds(pl.multiple_of(zz * 8, 8), 8), :], yz_v.at[z], 3, at(zz, x, src))
        return c

    lax.fori_loop(1, NZ, rows_z, 0)
    yz_v[z] = y128_v[pl.ds(pl.multiple_of(z * 8, 8), 8), :]

    drain(gz_v.at[pl.ds(0, NZ - 1)], recv_sem.at[2])
    raw8_v[...] = jnp.sum(gz_v[...], axis=0)
    gather_xs(raw8_v, gram1_v, 4)
    gram1_v[p] = raw8_v[...]

    def flip(k, c):
        xt_v[k] = x_v[k].T
        return c

    lax.fori_loop(0, SAMPLES, flip, 0)

    drain(gram1_v.at[pl.ds(0, NXS - 1)], recv_sem.at[4])
    a_v[...] = gram1_v[...].reshape(RANK, RANK) * gt_v[...] / (MIC_ALL * SAMPLES)
    invert(a_v)

    drain(yz_v.at[pl.ds(0, NZ - 1)], recv_sem.at[3])
    solved = exact_dot(jnp.sum(yz_v[...], axis=0), a_v[...])
    mine = pl.ds(pl.multiple_of(x * 128 + z * 8, 8), 8)
    raw_v[mine, :] = solved

    def back_z(d, c):
        zz = (z + d) % NZ
        send(raw_v.at[mine, :], raw_v.at[mine, :], 5, at(zz, x, src))
        return c

    lax.fori_loop(1, NZ, back_z, 0)
    drain(raw_v.at[pl.ds(0, 8 * (NZ - 1)), :], recv_sem.at[5])
    band = pl.ds(pl.multiple_of(x * 128, 128), 128)

    def back_x(d, c):
        xx = (x + d) % NX
        send(raw_v.at[band, :], raw_v.at[band, :], 6, at(z, xx, src))
        return c

    lax.fori_loop(1, NX, back_x, 0)
    drain(raw_v.at[pl.ds(0, 128 * (NX - 1)), :], recv_sem.at[6])

    raw = raw_v[...]
    gram2 = exact_dot(raw, raw, ((0,), (0,)))
    g2_v[...] = gram2

    def gram_s(d, c):
        ss = (src + d) % NSRC
        rows = pl.ds(pl.multiple_of(x * 64 + ss * 8, 8), 8)
        send(g2_v.at[rows, :], gs_v.at[src], 7, at(z, x, ss))
        return c

    lax.fori_loop(1, NSRC, gram_s, 0)
    gs_v[src] = g2_v[own_rows, :]

    for b in range(SRC_DEV // SRC_BLK):
        keep = blk_ref[b, 0].astype(F32)
        low_v[b * SRC_BLK : (b + 1) * SRC_BLK, :] = (
            raw_v[b * SRC_BLK : (b + 1) * SRC_BLK, :] * keep
        ).astype(BF16)

    def mic_part(kk, acc):
        low = low_v[...]
        left = xt_v[pl.ds(kk * 4, 4)].reshape(4 * MIC_DEV, SRC_DEV)
        prod = jnp.dot(left, low, preferred_element_type=F32)
        for i in range(4):
            piece = prod[i * MIC_DEV : (i + 1) * MIC_DEV, :]
            p_v[kk * 4 + i] = piece
            acc = acc + time_ref[pl.ds(kk * 4 + i, 1), :] * piece
        return acc

    mm_v[...] = lax.fori_loop(0, SAMPLES // 4, mic_part, jnp.zeros((MIC_DEV, RANK), F32))

    def mm_s(d, c):
        ss = (src + d) % NSRC
        rows = pl.ds(pl.multiple_of(ss * 16, 16), 16)
        send(mm_v.at[rows, :], mr_v.at[src], 8, at(z, x, ss))
        return c

    lax.fori_loop(1, NSRC, mm_s, 0)
    mic_rows = pl.ds(pl.multiple_of(src * 16, 16), 16)
    mr_v[src] = mm_v[mic_rows, :]

    drain(gs_v.at[pl.ds(0, NSRC - 1)], recv_sem.at[7])
    gs8_v[...] = jnp.sum(gs_v[...], axis=0)
    gather_xs(gs8_v, gram2_v, 9)
    gram2_v[p] = gs8_v[...]
    drain(gram2_v.at[pl.ds(0, NXS - 1)], recv_sem.at[9])
    gram_src = gram2_v[...].reshape(RANK, RANK)
    src_row, src_col = scales_of(gram_src, SRC_ALL)
    gram_src = gram_src / (src_row * src_col)
    gn_v[...] = gram_src
    a_v[...] = gram_src * gt_v[...] / (SRC_ALL * SAMPLES)
    src_out[...] = raw_v[...] / src_row
    invert(a_v)
    drain(mr_v.at[pl.ds(0, NSRC - 1)], recv_sem.at[8])
    right = jnp.sum(mr_v[...], axis=0) / src_row
    mraw_v[mic_rows, :] = exact_dot(right, a_v[...])

    def back_s(d, c):
        ss = (src + d) % NSRC
        send(mraw_v.at[mic_rows, :], mraw_v.at[mic_rows, :], 10, at(z, x, ss))
        return c

    lax.fori_loop(1, NSRC, back_s, 0)
    drain(mraw_v.at[pl.ds(0, 16 * (NSRC - 1)), :], recv_sem.at[10])

    mraw = mraw_v[...]
    g3_v[...] = exact_dot(mraw, mraw, ((0,), (0,)))

    def gram_x2(d, c):
        xx = (x + d) % NX
        rows = pl.ds(pl.multiple_of(xx * 64 + src * 8, 8), 8)
        send(g3_v.at[rows, :], hx_v.at[x], 11, at(z, xx, src))
        return c

    lax.fori_loop(1, NX, gram_x2, 0)
    hx_v[x] = g3_v[own_rows, :]

    def time_part(kb, c):
        rows = [
            jnp.sum(p_v[kb * 8 + i] * mraw_v[...], axis=0, keepdims=True) for i in range(8)
        ]
        piece = jnp.concatenate(rows, axis=0)
        t_v[kb] = piece[:, :128]
        t_v[kb + 4] = piece[:, 128:]
        return c

    lax.fori_loop(0, SAMPLES // 8, time_part, 0)

    def time_s(d, c):
        ss = (src + d) % NSRC
        send(t_v.at[ss], tr_v.at[src], 12, at(z, x, ss))
        return c

    lax.fori_loop(1, NSRC, time_s, 0)
    tr_v[src] = t_v[src]

    drain(hx_v.at[pl.ds(0, NX - 1)], recv_sem.at[11])
    drain(tr_v.at[pl.ds(0, NSRC - 1)], recv_sem.at[12])
    h_v[:, :RANK] = (hx_v[0] + hx_v[1]) + (hx_v[2] + hx_v[3])
    h_v[:, RANK:] = jnp.sum(tr_v[...], axis=0)

    zlo = z % 4
    zhi = z // 4

    def near(d, c):
        zz = zhi * 4 + (zlo + d) % 4
        send(h_v, hz_v.at[zlo], 13, at(zz, x, src))
        return c

    lax.fori_loop(1, 4, near, 0)
    hz_v[zlo] = h_v[...]
    drain(hz_v.at[pl.ds(0, 3)], recv_sem.at[13])
    h2_v[...] = (hz_v[0] + hz_v[1]) + (hz_v[2] + hz_v[3])

    def far(d, c):
        zz = ((zhi + d) % 4) * 4 + zlo
        send(h2_v, hy_v.at[zhi], 14, at(zz, x, src))
        return c

    lax.fori_loop(1, 4, far, 0)
    hy_v[zhi] = h2_v[...]
    drain(hy_v.at[pl.ds(0, 3)], recv_sem.at[14])
    h3_v[...] = (hy_v[0] + hy_v[1]) + (hy_v[2] + hy_v[3])
    gather_xs(h3_v, gram3_v, 15)
    gram3_v[p] = h3_v[...]
    drain(gram3_v.at[pl.ds(0, NXS - 1)], recv_sem.at[15])

    gram_mic = gram3_v[:, :, :RANK].reshape(RANK, RANK)
    mic_row, mic_col = scales_of(gram_mic, MIC_ALL)
    a_v[...] = gn_v[...] * (gram_mic / (mic_row * mic_col)) / (SRC_ALL * MIC_ALL)
    mic_out[...] = mraw_v[...] / mic_row
    invert(a_v)

    pieces = gram3_v[:, :, RANK:]
    parts = []
    for j in range(NSRC):
        parts.append((pieces[j] + pieces[8 + j]) + (pieces[16 + j] + pieces[24 + j]))
    total = jnp.concatenate(
        [jnp.concatenate([parts[kb], parts[kb + 4]], axis=1) for kb in range(4)], axis=0
    )
    total = total / (src_row * mic_row)
    time_raw = exact_dot(total, a_v[...])
    time_diag = jnp.sum(time_raw * time_raw, axis=0, keepdims=True)
    time_out[...] = time_raw / jnp.sqrt(time_diag / SAMPLES + 1e-06)

    drain(gx_v.at[pl.ds(0, NX - 1)], send_sem.at[0])
    drain(yx_v.at[pl.ds(0, NX - 1)], send_sem.at[1])
    drain(gz_v.at[pl.ds(0, NZ - 1)], send_sem.at[2])
    drain(yz_v.at[pl.ds(0, NZ - 1)], send_sem.at[3])
    drain(gram1_v.at[pl.ds(0, NXS - 1)], send_sem.at[4])
    drain(raw_v.at[pl.ds(0, 8 * (NZ - 1)), :], send_sem.at[5])
    drain(raw_v.at[pl.ds(0, 128 * (NX - 1)), :], send_sem.at[6])
    drain(gs_v.at[pl.ds(0, NSRC - 1)], send_sem.at[7])
    drain(mr_v.at[pl.ds(0, NSRC - 1)], send_sem.at[8])
    drain(gram2_v.at[pl.ds(0, NXS - 1)], send_sem.at[9])
    drain(mraw_v.at[pl.ds(0, 16 * (NSRC - 1)), :], send_sem.at[10])
    drain(hx_v.at[pl.ds(0, NX - 1)], send_sem.at[11])
    drain(tr_v.at[pl.ds(0, NSRC - 1)], send_sem.at[12])
    drain(hz_v.at[pl.ds(0, 3)], send_sem.at[13])
    drain(hy_v.at[pl.ds(0, 3)], send_sem.at[14])
    drain(gram3_v.at[pl.ds(0, NXS - 1)], send_sem.at[15])


def on_device(tensor_slab, observed_blocks, mic_factor, time_factor):
    vmem = pl.BlockSpec(memory_space=pltpu.VMEM)
    return pl.pallas_call(
        kernel,
        out_shape=(
            jax.ShapeDtypeStruct((SRC_DEV, RANK), F32),
            jax.ShapeDtypeStruct((MIC_DEV, RANK), F32),
            jax.ShapeDtypeStruct((SAMPLES, RANK), F32),
        ),
        in_specs=[
            pl.BlockSpec(memory_space=pl.ANY),
            pl.BlockSpec(memory_space=pltpu.SMEM),
            vmem,
            vmem,
        ],
        out_specs=(vmem, vmem, vmem),
        scratch_shapes=[
            pltpu.VMEM((SAMPLES, SRC_DEV, MIC_DEV), BF16),
            pltpu.VMEM((SAMPLES, MIC_DEV, SRC_DEV), BF16),
            pltpu.VMEM((SAMPLES * MIC_DEV, RANK), BF16),
            pltpu.VMEM((SAMPLES, MIC_DEV, RANK), F32),
            pltpu.VMEM((SRC_DEV, RANK), F32),
            pltpu.VMEM((NX, 128, RANK), F32),
            pltpu.VMEM((128, RANK), F32),
            pltpu.VMEM((NZ, 8, RANK), F32),
            pltpu.VMEM((8, RANK), F32),
            pltpu.VMEM((SRC_DEV, RANK), F32),
            pltpu.VMEM((SRC_DEV, RANK), BF16),
            pltpu.VMEM((RANK, RANK), F32),
            pltpu.VMEM((RANK, RANK), F32),
            pltpu.VMEM((RANK, RANK), F32),
            pltpu.VMEM((RANK, RANK), F32),
            pltpu.VMEM((NX, 8, RANK), F32),
            pltpu.VMEM((NZ, 8, RANK), F32),
            pltpu.VMEM((8, RANK), F32),
            pltpu.VMEM((NXS, 8, RANK), F32),
            pltpu.VMEM((RANK, RANK), F32),
            pltpu.VMEM((RANK, RANK), F32),
            pltpu.VMEM((NSRC, 8, RANK), F32),
            pltpu.VMEM((8, RANK), F32),
            pltpu.VMEM((NXS, 8, RANK), F32),
            pltpu.VMEM((MIC_DEV, RANK), F32),
            pltpu.VMEM((NSRC, 16, RANK), F32),
            pltpu.VMEM((MIC_DEV, RANK), F32),
            pltpu.VMEM((NSRC, 8, 128), F32),
            pltpu.VMEM((NSRC, 8, 128), F32),
            pltpu.VMEM((NX, 8, RANK), F32),
            pltpu.VMEM((8, RANK + 128), F32),
            pltpu.VMEM((4, 8, RANK + 128), F32),
            pltpu.VMEM((8, RANK + 128), F32),
            pltpu.VMEM((4, 8, RANK + 128), F32),
            pltpu.VMEM((8, RANK + 128), F32),
            pltpu.VMEM((NXS, 8, RANK + 128), F32),
            pltpu.SemaphoreType.DMA,
            pltpu.SemaphoreType.DMA((16,)),
            pltpu.SemaphoreType.DMA((16,)),
        ],
        compiler_params=pltpu.CompilerParams(
            collective_id=0, has_side_effects=True, vmem_limit_bytes=48 * 1024 * 1024
        ),
    )(tensor_slab, observed_blocks, mic_factor, time_factor)


def solution(mesh):
    placed = (P(None, "src", "mic"), P("src", "mic"), P("mic", None), P())
    return jax.shard_map(
        on_device,
        mesh=mesh,
        in_specs=placed,
        out_specs=(P("src", None), P("mic", None), P()),
        check_vma=False,
    )
```

```python
import functools

import jax
import jax.numpy as jnp
from jax import lax
from jax.experimental import pallas as pl
from jax.experimental.pallas import tpu as pltpu
from jax.sharding import PartitionSpec as P

MESH = pl.DeviceIdType.MESH
F32 = jnp.float32
BF16 = jnp.bfloat16

RANK = 256
SAMPLES = 32
SRC_DEV = 512
MIC_DEV = 128
SRC_BLK = 64
NX = 4
NZ = 16
NSRC = 8
NXS = NX * NSRC
SRC_ALL = SRC_DEV * NSRC
MIC_ALL = MIC_DEV * NX * NZ
BLK = 32
STAGES = 23


def exact_dot(a, b, dims=((1,), (0,))):
    return lax.dot_general(
        a, b, (dims, ((), ())), precision=lax.Precision.HIGHEST, preferred_element_type=F32
    )


def split3(a):
    first = a.astype(BF16)
    rest = a - first.astype(F32)
    second = rest.astype(BF16)
    third = (rest - second.astype(F32)).astype(BF16)
    return first, second, third


def outer_dot(a, b):
    a0, a1, a2 = split3(a)
    b0, b1, b2 = split3(b)
    left = jnp.concatenate([a0, a0, a1, a1, a0, a2], axis=0)
    right = jnp.concatenate([b0, b1, b0, b1, b2, b0], axis=0)
    return lax.dot_general(left, right, (((0,), (0,)), ((), ())), preferred_element_type=F32)


def twice(v):
    return jnp.concatenate([v, v], axis=1)


def eliminate(panel, rel, tile, first):
    sub = lax.broadcasted_iota(jnp.int32, (8, RANK), 0)
    sub_tile = lax.broadcasted_iota(jnp.int32, (8, 128), 0)
    groups = BLK // 8
    rows = [panel[8 * g : 8 * g + 8, :] for g in range(groups)]
    z_parts, w_parts = [], []
    for b in range(groups):
        lo = first + 8 * b
        col = {}
        for g in range(b, groups):
            part = rows[g][:, 128 * tile : 128 * tile + 128]
            col[g] = [jnp.broadcast_to(part[:, lo + j : lo + j + 1], (8, 128)) for j in range(8)]
        s = {}
        for k in range(8):
            for l in range(k, 8):
                s[k, l] = jnp.broadcast_to(col[b][l][k : k + 1, :], (8, 128))
        inside = (rel >= 8 * b) & (rel < 8 * b + 8)
        own = jnp.where(inside, jnp.where(rel == sub + 8 * b, -1.0, 0.0), rows[b])
        for g in range(b + 1, groups):
            rows[g] = jnp.where(inside, 0.0, rows[g])
        r = [jnp.broadcast_to(own[k : k + 1, :], (8, RANK)) for k in range(8)]
        inv = [None] * 8
        for j in range(0, 8, 2):
            a, m, d = s[j, j], s[j, j + 1], s[j + 1, j + 1]
            inv_det = 1.0 / (a * d - m * m)
            inv_a = 1.0 / a
            later = range(j + 2, 8)
            x = {l: s[j, l] for l in later}
            y = {l: s[j + 1, l] for l in later}
            u = {l: d * x[l] - m * y[l] for l in later}
            v = {l: a * y[l] - m * x[l] for l in later}
            for k in later:
                for l in range(k, 8):
                    s[k, l] = s[k, l] - (u[k] * x[l] + v[k] * y[l]) * inv_det
            f = m * inv_a
            r[j + 1] = r[j + 1] - twice(f) * r[j]
            inv[j] = inv_a
            inv[j + 1] = a * inv_det
            for k in later:
                r[k] = r[k] - twice(x[k] * inv_a) * r[j] - twice(v[k] * inv_det) * r[j + 1]
            for g in range(b + 1, groups):
                c1 = (col[g][j + 1] - col[g][j] * f) * inv[j + 1]
                c0 = col[g][j] * inv_a
                rows[g] = rows[g] - twice(c0) * r[j] - twice(c1) * r[j + 1]
                for l in later:
                    col[g][l] = col[g][l] - c0 * x[l] - c1 * (v[l] * inv_a)
        z, w = r[0], inv[0]
        for k in range(1, 8):
            z = jnp.where(sub == k, r[k], z)
            w = jnp.where(sub_tile == k, inv[k], w)
        z = jnp.where((rel >= 8 * b + 8) & (rel < BLK), 0.0, z)
        z_parts.append(z)
        w_parts.append(z * twice(w))
    return jnp.concatenate(z_parts, axis=0), jnp.concatenate(w_parts, axis=0)


def invert_block(a_ref, i):
    lane = lax.broadcasted_iota(jnp.int32, (8, RANK), 1)
    lane_row = lax.broadcasted_iota(jnp.int32, (1, RANK), 1)
    base = i * BLK
    rows = slice(base, base + BLK)
    z, w = eliminate(a_ref[rows, :], lane - base, base // 128, base % 128)
    inside = (lane_row >= base) & (lane_row < base + BLK)
    update = outer_dot(z, w)
    a_ref[rows, :] = jnp.zeros((BLK, RANK), F32)
    a_ref[...] = jnp.where(inside, 0.0, a_ref[...]) - update


def invert(a_ref, between=None):
    for i in range(RANK // BLK):
        invert_block(a_ref, i)
        if between is not None and i in between:
            between[i]()


def diagonal(gram):
    rows = lax.broadcasted_iota(jnp.int32, (RANK, RANK), 0)
    cols = lax.broadcasted_iota(jnp.int32, (RANK, RANK), 1)
    only = jnp.where(rows == cols, gram, 0.0)
    return jnp.sum(only, axis=0, keepdims=True), jnp.sum(only, axis=1, keepdims=True)


def scales_of(gram, count):
    row, col = diagonal(gram)
    return jnp.sqrt(row / count + 1e-06), jnp.sqrt(col / count + 1e-06)


def drain(ref, sem):
    pltpu.make_async_copy(ref, ref, sem).wait()


def ring_step(i):
    half = (i + 1) // 2
    return NZ // 2 + half - 2 * half * (i % 2)


def eight(k):
    return pl.ds(pl.multiple_of(k * 8, 8), 8)


def sweep(
    x_hbm,
    blk_hbm,
    mic_hbm,
    time_hbm,
    src_out,
    mic_out,
    time_out,
    blk_ref,
    mic_ref,
    time_ref,
    x_v,
    xt_v,
    kr_v,
    p_v,
    y_v,
    yx_v,
    y128_v,
    yz_v,
    yall_v,
    raw_v,
    low_v,
    gt_v,
    a_v,
    gn_v,
    g1_v,
    g1x_v,
    g1s_v,
    g1z_v,
    g1p_v,
    g1a_v,
    g2_v,
    g2s_v,
    g2p_v,
    g2a_v,
    mm_v,
    mr_v,
    mall_v,
    mraw_v,
    g3_v,
    g3x_v,
    g3s_v,
    g3z_v,
    g3p_v,
    g3a_v,
    t_v,
    ts_v,
    tp_v,
    tz_v,
    tq_v,
    ta_v,
    load_sem,
    send_sem,
    recv_sem,
):
    me_mic = lax.axis_index("mic")
    src = lax.axis_index("src")
    z = me_mic // NX
    x = me_mic % NX
    p = x * NSRC + src

    def at(zz, xx, ss):
        return (zz * NX + xx, ss)

    load_mic = pltpu.make_async_copy(mic_hbm, mic_ref, load_sem.at[0])
    load_time = pltpu.make_async_copy(time_hbm, time_ref, load_sem.at[1])
    load_blk = pltpu.make_async_copy(blk_hbm, blk_ref, load_sem.at[2])
    load = pltpu.make_async_copy(x_hbm, x_v, load_sem.at[3])
    load_mic.start()
    load_time.start()
    load_blk.start()
    load.start()

    barrier = pltpu.get_barrier_semaphore()

    def greet_z(d, c):
        pl.semaphore_signal(barrier, inc=1, device_id=at((z + d) % NZ, x, src), device_id_type=MESH)
        return c

    def greet_xs(d, c):
        q = (p + d) % NXS
        pl.semaphore_signal(
            barrier, inc=1, device_id=at(z, q // NSRC, q % NSRC), device_id_type=MESH
        )
        return c

    lax.fori_loop(1, NZ, greet_z, 0)
    lax.fori_loop(1, NXS, greet_xs, 0)

    waiting = {}

    def expect(stage, ref):
        waiting[stage] = [ref, True]

    def arrived(stage):
        drain(waiting[stage][0], recv_sem.at[stage])
        waiting[stage][1] = False

    def send(src_ref, dst_ref, stage, device):
        pltpu.make_async_remote_copy(
            src_ref=src_ref,
            dst_ref=dst_ref,
            send_sem=send_sem.at[stage],
            recv_sem=recv_sem.at[stage],
            device_id=device,
            device_id_type=MESH,
        ).start()

    def send_x(gram_ref, dst, stage):
        expect(stage, dst.at[pl.ds(0, NX - 1)])

        def one(d, c):
            xx = (x + d) % NX
            send(gram_ref.at[eight(xx * NSRC + src), :], dst.at[x], stage, at(z, xx, src))
            return c

        lax.fori_loop(1, NX, one, 0)
        dst[x] = gram_ref[eight(p), :]

    def send_z(piece_ref, dst, stage):
        expect(stage, dst.at[pl.ds(0, NZ - 1)])

        def one(i, c):
            send(piece_ref, dst.at[z], stage, at((z + ring_step(i)) % NZ, x, src))
            return c

        lax.fori_loop(0, NZ - 1, one, 0)
        dst[z] = piece_ref[...]

    def send_xs(piece_ref, dst, stage):
        expect(stage, dst.at[pl.ds(0, NXS - 1)])

        def one(d, c):
            q = (p + d) % NXS
            send(piece_ref, dst.at[p], stage, at(z, q // NSRC, q % NSRC))
            return c

        lax.fori_loop(1, NXS, one, 0)
        dst[p] = piece_ref[...]

    def send_src(piece_of, dst_ref, expected, stage):
        expect(stage, expected)

        def one(d, c):
            ss = (src + d) % NSRC
            send(piece_of(ss), dst_ref, stage, at(z, x, ss))
            return c

        lax.fori_loop(1, NSRC, one, 0)

    load_mic.wait()
    load_time.wait()
    mic = mic_ref[...]
    g1_v[...] = exact_dot(mic, mic, ((0,), (0,)))
    times = time_ref[...]
    gt_v[...] = exact_dot(times, times, ((0,), (0,)))
    mic_low = mic.astype(BF16).astype(F32)

    def make_kr(k, c):
        kr_v[pl.ds(pl.multiple_of(k * MIC_DEV, MIC_DEV), MIC_DEV), :] = (
            time_ref[pl.ds(k, 1), :] * mic_low
        ).astype(BF16)
        return c

    lax.fori_loop(0, SAMPLES, make_kr, 0)

    load_blk.wait()
    load.wait()
    for xx in range(NX):
        left = jnp.concatenate(
            [x_v[k, xx * 128 : (xx + 1) * 128, :] for k in range(SAMPLES)], axis=1
        )
        part = jnp.dot(left, kr_v[...], preferred_element_type=F32)
        for h in range(2):
            keep = blk_ref[0, xx * 2 + h].astype(F32)
            rows = slice(xx * 128 + h * 64, xx * 128 + (h + 1) * 64)
            y_v[rows, :] = part[h * 64 : (h + 1) * 64, :] * keep

    pl.semaphore_wait(barrier, NZ - 1 + NXS - 1)
    yield waiting

    send_x(g1_v, g1x_v, 0)

    for g in range(4):
        expect(3 + g, yx_v.at[0, pl.ds(0, 96), :])

        def row_group(dx, c, g=g):
            xx = (x + dx) % NX

            def one(i, c):
                zz = (z + ring_step(i)) % NZ
                send(
                    y_v.at[eight(xx * NZ + zz), :],
                    yx_v.at[dx - 1, eight(zz), :],
                    3 + g,
                    at(z, xx, src),
                )
                return c

            return lax.fori_loop(4 * g, 4 * g + 4, one, c)

        lax.fori_loop(1, NX, row_group, 0)

    arrived(0)
    g1s_v[...] = (g1x_v[0] + g1x_v[1]) + (g1x_v[2] + g1x_v[3])
    send_z(g1s_v, g1z_v, 1)

    expect(7, yz_v.at[pl.ds(0, NZ - 1)])
    for g in range(4):
        arrived(3 + g)

        def sum_send(i, c):
            zz = (z + ring_step(i)) % NZ
            rows = eight(zz)
            y128_v[rows, :] = (y_v[eight(x * NZ + zz), :] + yx_v[0, rows, :]) + (
                yx_v[1, rows, :] + yx_v[2, rows, :]
            )
            send(y128_v.at[rows, :], yz_v.at[i], 7, at(zz, x, src))
            return c

        lax.fori_loop(4 * g, min(4 * g + 4, NZ - 1), sum_send, 0)
    own = eight(z)
    yz_v[NZ - 1] = (y_v[eight(x * NZ + z), :] + yx_v[0, own, :]) + (
        yx_v[1, own, :] + yx_v[2, own, :]
    )
    yield waiting

    def flip(k, c):
        xt_v[k] = x_v[k].T
        return c

    lax.fori_loop(0, SAMPLES, flip, 0)

    arrived(7)
    mine = eight(x * NZ + z)
    yall_v[mine, :] = jnp.sum(yz_v[...], axis=0)
    for g in range(4):
        last = min(4 * g + 4, NZ - 1)
        expect(8 + g, yall_v.at[pl.ds(0, 8 * (last - 4 * g)), :])

        def back_z(i, c, g=g):
            zz = (z + ring_step(i)) % NZ
            send(yall_v.at[mine, :], yall_v.at[mine, :], 8 + g, at(zz, x, src))
            return c

        lax.fori_loop(4 * g, last, back_z, 0)

    expect(12, yall_v.at[pl.ds(0, 128 * (NX - 1)), :])

    def forward(rows):
        def one(dx, c):
            send(yall_v.at[rows, :], yall_v.at[rows, :], 12, at(z, (x + dx) % NX, src))
            return c

        lax.fori_loop(1, NX, one, 0)

    def forward_group(g):
        arrived(8 + g)

        def one(i, c):
            forward(eight(x * NZ + (z + NZ - ring_step(i)) % NZ))
            return c

        lax.fori_loop(4 * g, min(4 * g + 4, NZ - 1), one, 0)

    forward(mine)
    yield waiting

    arrived(1)
    g1p_v[...] = jnp.sum(g1z_v[...], axis=0)
    send_xs(g1p_v, g1a_v, 2)
    forward_group(3)
    forward_group(2)
    arrived(2)
    yield waiting
    a_v[...] = g1a_v[...].reshape(RANK, RANK) * gt_v[...] * (1.0 / (MIC_ALL * SAMPLES))
    invert(a_v, {1: lambda: forward_group(1), 3: lambda: forward_group(0)})
    yield waiting
    arrived(12)
    yield waiting
    raw = -exact_dot(yall_v[...], a_v[...])
    raw_v[...] = raw

    g2_v[...] = exact_dot(raw, raw, ((0,), (0,)))
    send_src(
        lambda ss: g2_v.at[eight(x * NSRC + ss), :],
        g2s_v.at[src],
        g2s_v.at[pl.ds(0, NSRC - 1)],
        13,
    )
    g2s_v[src] = g2_v[eight(p), :]

    for b in range(SRC_DEV // SRC_BLK):
        keep = blk_ref[0, b].astype(F32)
        rows = slice(b * SRC_BLK, (b + 1) * SRC_BLK)
        low_v[rows, :] = (raw_v[rows, :] * keep).astype(BF16)

    def mic_part(kk, acc):
        left = xt_v[pl.ds(kk * 8, 8)].reshape(8 * MIC_DEV, SRC_DEV)
        prod = jnp.dot(left, low_v[...], preferred_element_type=F32)
        for i in range(8):
            piece = prod[i * MIC_DEV : (i + 1) * MIC_DEV, :]
            p_v[kk * 8 + i] = piece
            acc = acc + time_ref[pl.ds(kk * 8 + i, 1), :] * piece
        return acc

    mm_v[...] = lax.fori_loop(0, SAMPLES // 8, mic_part, jnp.zeros((MIC_DEV, RANK), F32))

    def sixteen(k):
        return pl.ds(pl.multiple_of(k * 16, 16), 16)

    mic_rows = sixteen(src)
    send_src(
        lambda ss: mm_v.at[sixteen(ss), :], mr_v.at[src], mr_v.at[pl.ds(0, NSRC - 1)], 15
    )
    mr_v[src] = mm_v[mic_rows, :]
    yield waiting
    arrived(13)
    g2p_v[...] = jnp.sum(g2s_v[...], axis=0)
    send_xs(g2p_v, g2a_v, 14)
    arrived(15)
    mall_v[mic_rows, :] = jnp.sum(mr_v[...], axis=0)
    send_src(
        lambda ss: mall_v.at[mic_rows, :],
        mall_v.at[mic_rows, :],
        mall_v.at[pl.ds(0, 16 * (NSRC - 1)), :],
        16,
    )
    arrived(14)
    yield waiting
    gram_src = g2a_v[...].reshape(RANK, RANK)
    src_row, src_col = scales_of(gram_src, SRC_ALL)
    gram_src = gram_src / (src_row * src_col)
    gn_v[...] = gram_src
    a_v[...] = gram_src * gt_v[...] * (1.0 / (SRC_ALL * SAMPLES))
    invert(a_v)
    yield waiting
    arrived(16)
    mraw = -exact_dot(mall_v[...] / src_row, a_v[...])
    mraw_v[...] = mraw

    g3_v[...] = exact_dot(mraw, mraw, ((0,), (0,)))
    send_x(g3_v, g3x_v, 17)

    def time_part(kb, c):
        rows = [jnp.sum(p_v[kb * 8 + i] * mraw_v[...], axis=0, keepdims=True) for i in range(8)]
        piece = jnp.concatenate(rows, axis=0)
        t_v[kb] = piece[:, :128]
        t_v[kb + 4] = piece[:, 128:]
        return c

    lax.fori_loop(0, SAMPLES // 8, time_part, 0)
    send_src(lambda ss: t_v.at[ss], ts_v.at[src], ts_v.at[pl.ds(0, NSRC - 1)], 20)
    ts_v[src] = t_v[src]
    yield waiting

    arrived(17)
    g3s_v[...] = (g3x_v[0] + g3x_v[1]) + (g3x_v[2] + g3x_v[3])
    send_z(g3s_v, g3z_v, 18)
    arrived(20)
    tp_v[...] = jnp.sum(ts_v[...], axis=0)
    send_z(tp_v, tz_v, 21)
    src_out[...] = raw_v[...] / src_row
    arrived(18)
    yield waiting
    g3p_v[...] = jnp.sum(g3z_v[...], axis=0)
    send_xs(g3p_v, g3a_v, 19)
    arrived(21)
    tq_v[...] = jnp.sum(tz_v[...], axis=0)
    send_xs(tq_v, ta_v, 22)
    arrived(19)
    yield waiting

    gram_mic = g3a_v[...].reshape(RANK, RANK)
    mic_row, mic_col = scales_of(gram_mic, MIC_ALL)
    a_v[...] = gn_v[...] * (gram_mic / (mic_row * mic_col)) * (1.0 / (SRC_ALL * MIC_ALL))
    mic_out[...] = mraw_v[...] / mic_row
    invert(a_v)
    yield waiting

    arrived(22)
    parts = []
    for j in range(NSRC):
        parts.append((ta_v[j] + ta_v[8 + j]) + (ta_v[16 + j] + ta_v[24 + j]))
    total = jnp.concatenate(
        [jnp.concatenate([parts[kb], parts[kb + 4]], axis=1) for kb in range(4)], axis=0
    )
    total = total / (src_row * mic_row)
    time_raw = -exact_dot(total, a_v[...])
    time_diag = jnp.sum(time_raw * time_raw, axis=0, keepdims=True)
    time_out[...] = time_raw / jnp.sqrt(time_diag / SAMPLES + 1e-06)

    yield waiting


def kernel(*refs, stop=None):
    send_sem, recv_sem = refs[-2:]
    for count, waiting in enumerate(sweep(*refs)):
        if count == stop:
            break
    for stage, (ref, coming) in waiting.items():
        if coming:
            drain(ref, recv_sem.at[stage])
        drain(ref, send_sem.at[stage])


def on_device(tensor_slab, observed_blocks, mic_factor, time_factor, stop=None, collective_id=0, name=None):
    vmem = pl.BlockSpec(memory_space=pltpu.VMEM)
    return pl.pallas_call(
        functools.partial(kernel, stop=stop),
        name=name,
        out_shape=(
            jax.ShapeDtypeStruct((SRC_DEV, RANK), F32),
            jax.ShapeDtypeStruct((MIC_DEV, RANK), F32),
            jax.ShapeDtypeStruct((SAMPLES, RANK), F32),
        ),
        in_specs=[pl.BlockSpec(memory_space=pltpu.HBM)] * 4,
        out_specs=(vmem, vmem, vmem),
        scratch_shapes=[
            pltpu.SMEM((1, SRC_DEV // SRC_BLK), jnp.int32),
            pltpu.VMEM((MIC_DEV, RANK), F32),
            pltpu.VMEM((SAMPLES, RANK), F32),
            pltpu.VMEM((SAMPLES, SRC_DEV, MIC_DEV), BF16),
            pltpu.VMEM((SAMPLES, MIC_DEV, SRC_DEV), BF16),
            pltpu.VMEM((SAMPLES * MIC_DEV, RANK), BF16),
            pltpu.VMEM((SAMPLES, MIC_DEV, RANK), F32),
            pltpu.VMEM((SRC_DEV, RANK), F32),
            pltpu.VMEM((NX - 1, 128, RANK), F32),
            pltpu.VMEM((128, RANK), F32),
            pltpu.VMEM((NZ, 8, RANK), F32),
            pltpu.VMEM((SRC_DEV, RANK), F32),
            pltpu.VMEM((SRC_DEV, RANK), F32),
            pltpu.VMEM((SRC_DEV, RANK), BF16),
            pltpu.VMEM((RANK, RANK), F32),
            pltpu.VMEM((RANK, RANK), F32),
            pltpu.VMEM((RANK, RANK), F32),
            pltpu.VMEM((RANK, RANK), F32),
            pltpu.VMEM((NX, 8, RANK), F32),
            pltpu.VMEM((8, RANK), F32),
            pltpu.VMEM((NZ, 8, RANK), F32),
            pltpu.VMEM((8, RANK), F32),
            pltpu.VMEM((NXS, 8, RANK), F32),
            pltpu.VMEM((RANK, RANK), F32),
            pltpu.VMEM((NSRC, 8, RANK), F32),
            pltpu.VMEM((8, RANK), F32),
            pltpu.VMEM((NXS, 8, RANK), F32),
            pltpu.VMEM((MIC_DEV, RANK), F32),
            pltpu.VMEM((NSRC, 16, RANK), F32),
            pltpu.VMEM((MIC_DEV, RANK), F32),
            pltpu.VMEM((MIC_DEV, RANK), F32),
            pltpu.VMEM((RANK, RANK), F32),
            pltpu.VMEM((NX, 8, RANK), F32),
            pltpu.VMEM((8, RANK), F32),
            pltpu.VMEM((NZ, 8, RANK), F32),
            pltpu.VMEM((8, RANK), F32),
            pltpu.VMEM((NXS, 8, RANK), F32),
            pltpu.VMEM((NSRC, 8, 128), F32),
            pltpu.VMEM((NSRC, 8, 128), F32),
            pltpu.VMEM((8, 128), F32),
            pltpu.VMEM((NZ, 8, 128), F32),
            pltpu.VMEM((8, 128), F32),
            pltpu.VMEM((NXS, 8, 128), F32),
            pltpu.SemaphoreType.DMA((4,)),
            pltpu.SemaphoreType.DMA((STAGES,)),
            pltpu.SemaphoreType.DMA((STAGES,)),
        ],
        compiler_params=pltpu.CompilerParams(
            collective_id=collective_id, has_side_effects=True, vmem_limit_bytes=60 * 1024 * 1024
        ),
    )(tensor_slab, observed_blocks.reshape(1, SRC_DEV // SRC_BLK), mic_factor, time_factor)


def solution(mesh):
    placed = (P(None, "src", "mic"), P("src", "mic"), P("mic", None), P())
    return jax.shard_map(
        on_device,
        mesh=mesh,
        in_specs=placed,
        out_specs=(P("src", None), P("mic", None), P()),
        check_vma=False,
    )
```

```python
import functools

import jax
import jax.numpy as jnp
from jax import lax
from jax.experimental import pallas as pl
from jax.experimental.pallas import tpu as pltpu
from jax.sharding import PartitionSpec as P

MESH = pl.DeviceIdType.MESH
F32 = jnp.float32
BF16 = jnp.bfloat16

RANK = 256
SAMPLES = 32
SRC_DEV = 512
MIC_DEV = 128
SRC_BLK = 64
NX = 4
NZ = 16
NSRC = 8
NXS = NX * NSRC
SRC_ALL = SRC_DEV * NSRC
MIC_ALL = MIC_DEV * NX * NZ
BLK = 32
STAGES = 23


def exact_dot(a, b, dims=((1,), (0,))):
    return lax.dot_general(
        a, b, (dims, ((), ())), precision=lax.Precision.HIGHEST, preferred_element_type=F32
    )


def split3(a):
    first = a.astype(BF16)
    rest = a - first.astype(F32)
    second = rest.astype(BF16)
    third = (rest - second.astype(F32)).astype(BF16)
    return first, second, third


def outer_dot(a, b):
    a0, a1, a2 = split3(a)
    b0, b1, b2 = split3(b)
    left = jnp.concatenate([a0, a0, a1, a1, a0, a2], axis=0)
    right = jnp.concatenate([b0, b1, b0, b1, b2, b0], axis=0)
    return lax.dot_general(left, right, (((0,), (0,)), ((), ())), preferred_element_type=F32)


def twice(v):
    return jnp.concatenate([v, v], axis=1)


def eliminate(panel, rel, tile, first):
    sub = lax.broadcasted_iota(jnp.int32, (8, RANK), 0)
    sub_tile = lax.broadcasted_iota(jnp.int32, (8, 128), 0)
    groups = BLK // 8
    rows = [panel[8 * g : 8 * g + 8, :] for g in range(groups)]
    z_parts, w_parts = [], []
    for b in range(groups):
        lo = first + 8 * b
        col = {}
        for g in range(b, groups):
            part = rows[g][:, 128 * tile : 128 * tile + 128]
            col[g] = [jnp.broadcast_to(part[:, lo + j : lo + j + 1], (8, 128)) for j in range(8)]
        s = {}
        for k in range(8):
            for l in range(k, 8):
                s[k, l] = jnp.broadcast_to(col[b][l][k : k + 1, :], (8, 128))
        inside = (rel >= 8 * b) & (rel < 8 * b + 8)
        own = jnp.where(inside, jnp.where(rel == sub + 8 * b, -1.0, 0.0), rows[b])
        for g in range(b + 1, groups):
            rows[g] = jnp.where(inside, 0.0, rows[g])
        r = [jnp.broadcast_to(own[k : k + 1, :], (8, RANK)) for k in range(8)]
        inv = [None] * 8
        for j in range(0, 8, 2):
            a, m, d = s[j, j], s[j, j + 1], s[j + 1, j + 1]
            inv_det = 1.0 / (a * d - m * m)
            inv_a = 1.0 / a
            later = range(j + 2, 8)
            x = {l: s[j, l] for l in later}
            y = {l: s[j + 1, l] for l in later}
            u = {l: d * x[l] - m * y[l] for l in later}
            v = {l: a * y[l] - m * x[l] for l in later}
            for k in later:
                for l in range(k, 8):
                    s[k, l] = s[k, l] - (u[k] * x[l] + v[k] * y[l]) * inv_det
            f = m * inv_a
            r[j + 1] = r[j + 1] - twice(f) * r[j]
            inv[j] = inv_a
            inv[j + 1] = a * inv_det
            for k in later:
                r[k] = r[k] - twice(x[k] * inv_a) * r[j] - twice(v[k] * inv_det) * r[j + 1]
            for g in range(b + 1, groups):
                c1 = (col[g][j + 1] - col[g][j] * f) * inv[j + 1]
                c0 = col[g][j] * inv_a
                rows[g] = rows[g] - twice(c0) * r[j] - twice(c1) * r[j + 1]
                for l in later:
                    col[g][l] = col[g][l] - c0 * x[l] - c1 * (v[l] * inv_a)
        z, w = r[0], inv[0]
        for k in range(1, 8):
            z = jnp.where(sub == k, r[k], z)
            w = jnp.where(sub_tile == k, inv[k], w)
        z = jnp.where((rel >= 8 * b + 8) & (rel < BLK), 0.0, z)
        z_parts.append(z)
        w_parts.append(z * twice(w))
    return jnp.concatenate(z_parts, axis=0), jnp.concatenate(w_parts, axis=0)


def invert_block(a_ref, i):
    lane = lax.broadcasted_iota(jnp.int32, (8, RANK), 1)
    lane_row = lax.broadcasted_iota(jnp.int32, (1, RANK), 1)
    base = i * BLK
    rows = slice(base, base + BLK)
    z, w = eliminate(a_ref[rows, :], lane - base, base // 128, base % 128)
    inside = (lane_row >= base) & (lane_row < base + BLK)
    update = outer_dot(z, w)
    a_ref[rows, :] = jnp.zeros((BLK, RANK), F32)
    a_ref[...] = jnp.where(inside, 0.0, a_ref[...]) - update


def invert(a_ref, between=None):
    for i in range(RANK // BLK):
        invert_block(a_ref, i)
        if between is not None and i in between:
            between[i]()


def diagonal(gram):
    rows = lax.broadcasted_iota(jnp.int32, (RANK, RANK), 0)
    cols = lax.broadcasted_iota(jnp.int32, (RANK, RANK), 1)
    only = jnp.where(rows == cols, gram, 0.0)
    return jnp.sum(only, axis=0, keepdims=True), jnp.sum(only, axis=1, keepdims=True)


def scales_of(gram, count):
    row, col = diagonal(gram)
    return jnp.sqrt(row / count + 1e-06), jnp.sqrt(col / count + 1e-06)


def drain(ref, sem):
    pltpu.make_async_copy(ref, ref, sem).wait()


def ring_step(i):
    half = (i + 1) // 2
    return NZ // 2 + half - 2 * half * (i % 2)


def eight(k):
    return pl.ds(pl.multiple_of(k * 8, 8), 8)


def sweep(
    x_hbm,
    blk_hbm,
    mic_hbm,
    time_hbm,
    src_out,
    mic_out,
    time_out,
    blk_ref,
    mic_ref,
    time_ref,
    x_v,
    xt_v,
    kr_v,
    p_v,
    y_v,
    yx_v,
    y128_v,
    yz_v,
    yall_v,
    raw_v,
    low_v,
    gt_v,
    a_v,
    gn_v,
    g1_v,
    g1x_v,
    g1s_v,
    g1z_v,
    g1p_v,
    g1a_v,
    g2_v,
    g2s_v,
    g2p_v,
    g2a_v,
    mm_v,
    mr_v,
    m16_v,
    mall_v,
    mraw_v,
    g3_v,
    g3s_v,
    g3z_v,
    g3p_v,
    g3a_v,
    t_v,
    ts_v,
    tp_v,
    tz_v,
    tq_v,
    ta_v,
    time_v,
    load_sem,
    send_sem,
    recv_sem,
):
    me_mic = lax.axis_index("mic")
    src = lax.axis_index("src")
    z = me_mic // NX
    x = me_mic % NX
    p = x * NSRC + src

    def at(zz, xx, ss):
        return (zz * NX + xx, ss)

    load_mic = pltpu.make_async_copy(mic_hbm, mic_ref, load_sem.at[0])
    load_time = pltpu.make_async_copy(time_hbm, time_ref, load_sem.at[1])
    load_blk = pltpu.make_async_copy(blk_hbm, blk_ref, load_sem.at[2])
    load = pltpu.make_async_copy(x_hbm, x_v, load_sem.at[3])
    load_mic.start()
    load_time.start()
    load_blk.start()
    load.start()

    barrier = pltpu.get_barrier_semaphore()

    def greet_z(d, c):
        pl.semaphore_signal(barrier, inc=1, device_id=at((z + d) % NZ, x, src), device_id_type=MESH)
        return c

    def greet_xs(d, c):
        q = (p + d) % NXS
        pl.semaphore_signal(
            barrier, inc=1, device_id=at(z, q // NSRC, q % NSRC), device_id_type=MESH
        )
        return c

    lax.fori_loop(1, NZ, greet_z, 0)
    lax.fori_loop(1, NXS, greet_xs, 0)

    waiting = {}

    def expect(stage, ref):
        waiting[stage] = [ref, True]

    def arrived(stage):
        drain(waiting[stage][0], recv_sem.at[stage])
        waiting[stage][1] = False

    def send(src_ref, dst_ref, stage, device):
        pltpu.make_async_remote_copy(
            src_ref=src_ref,
            dst_ref=dst_ref,
            send_sem=send_sem.at[stage],
            recv_sem=recv_sem.at[stage],
            device_id=device,
            device_id_type=MESH,
        ).start()

    def send_x(gram_ref, dst, stage):
        expect(stage, dst.at[pl.ds(0, NX - 1)])

        def one(d, c):
            xx = (x + d) % NX
            send(gram_ref.at[eight(xx * NSRC + src), :], dst.at[x], stage, at(z, xx, src))
            return c

        lax.fori_loop(1, NX, one, 0)
        dst[x] = gram_ref[eight(p), :]

    def send_z(piece_ref, dst, stage):
        expect(stage, dst.at[pl.ds(0, NZ - 1)])

        def one(i, c):
            send(piece_ref, dst.at[z], stage, at((z + ring_step(i)) % NZ, x, src))
            return c

        lax.fori_loop(0, NZ - 1, one, 0)
        dst[z] = piece_ref[...]

    def send_xs(piece_ref, dst, stage):
        expect(stage, dst.at[pl.ds(0, NXS - 1)])

        def one(d, c):
            q = (p + d) % NXS
            send(piece_ref, dst.at[p], stage, at(z, q // NSRC, q % NSRC))
            return c

        lax.fori_loop(1, NXS, one, 0)
        dst[p] = piece_ref[...]

    def send_src(piece_of, dst_ref, expected, stage):
        expect(stage, expected)

        def one(d, c):
            ss = (src + d) % NSRC
            send(piece_of(ss), dst_ref, stage, at(z, x, ss))
            return c

        lax.fori_loop(1, NSRC, one, 0)

    load_mic.wait()
    load_time.wait()
    mic = mic_ref[...]
    g1_v[...] = exact_dot(mic, mic, ((0,), (0,)))
    times = time_ref[...]
    gt_v[...] = exact_dot(times, times, ((0,), (0,)))
    mic_low = mic.astype(BF16).astype(F32)

    def make_kr(k, c):
        kr_v[pl.ds(pl.multiple_of(k * MIC_DEV, MIC_DEV), MIC_DEV), :] = (
            time_ref[pl.ds(k, 1), :] * mic_low
        ).astype(BF16)
        return c

    lax.fori_loop(0, SAMPLES, make_kr, 0)

    load_blk.wait()
    load.wait()
    for xx in range(NX):
        left = jnp.concatenate(
            [x_v[k, xx * 128 : (xx + 1) * 128, :] for k in range(SAMPLES)], axis=1
        )
        part = jnp.dot(left, kr_v[...], preferred_element_type=F32)
        for h in range(2):
            keep = blk_ref[0, xx * 2 + h].astype(F32)
            rows = slice(xx * 128 + h * 64, xx * 128 + (h + 1) * 64)
            y_v[rows, :] = part[h * 64 : (h + 1) * 64, :] * keep

    pl.semaphore_wait(barrier, NZ - 1 + NXS - 1)
    yield waiting

    send_x(g1_v, g1x_v, 0)

    for g in range(4):
        expect(3 + g, yx_v.at[0, pl.ds(0, 96), :])

        def row_group(dx, c, g=g):
            xx = (x + dx) % NX

            def one(i, c):
                zz = (z + ring_step(i)) % NZ
                send(
                    y_v.at[eight(xx * NZ + zz), :],
                    yx_v.at[dx - 1, eight(zz), :],
                    3 + g,
                    at(z, xx, src),
                )
                return c

            return lax.fori_loop(4 * g, 4 * g + 4, one, c)

        lax.fori_loop(1, NX, row_group, 0)

    arrived(0)
    g1s_v[...] = (g1x_v[0] + g1x_v[1]) + (g1x_v[2] + g1x_v[3])
    send_z(g1s_v, g1z_v, 1)

    expect(7, yz_v.at[pl.ds(0, NZ - 1)])
    for g in range(4):
        arrived(3 + g)

        def sum_send(i, c):
            zz = (z + ring_step(i)) % NZ
            rows = eight(zz)
            y128_v[rows, :] = (y_v[eight(x * NZ + zz), :] + yx_v[0, rows, :]) + (
                yx_v[1, rows, :] + yx_v[2, rows, :]
            )
            send(y128_v.at[rows, :], yz_v.at[i], 7, at(zz, x, src))
            return c

        lax.fori_loop(4 * g, min(4 * g + 4, NZ - 1), sum_send, 0)
    own = eight(z)
    yz_v[NZ - 1] = (y_v[eight(x * NZ + z), :] + yx_v[0, own, :]) + (
        yx_v[1, own, :] + yx_v[2, own, :]
    )
    yield waiting

    arrived(1)
    g1p_v[...] = jnp.sum(g1z_v[...], axis=0)
    send_xs(g1p_v, g1a_v, 2)

    arrived(7)
    mine = eight(x * NZ + z)
    yall_v[mine, :] = jnp.sum(yz_v[...], axis=0)
    for g in range(4):
        last = min(4 * g + 4, NZ - 1)
        expect(8 + g, yall_v.at[pl.ds(0, 8 * (last - 4 * g)), :])

        def back_z(i, c, g=g):
            zz = (z + ring_step(i)) % NZ
            send(yall_v.at[mine, :], yall_v.at[mine, :], 8 + g, at(zz, x, src))
            return c

        lax.fori_loop(4 * g, last, back_z, 0)

    expect(12, yall_v.at[pl.ds(0, 128 * (NX - 1)), :])

    def forward(rows):
        def one(dx, c):
            send(yall_v.at[rows, :], yall_v.at[rows, :], 12, at(z, (x + dx) % NX, src))
            return c

        lax.fori_loop(1, NX, one, 0)

    def forward_group(g):
        arrived(8 + g)

        def one(i, c):
            forward(eight(x * NZ + (z + NZ - ring_step(i)) % NZ))
            return c

        lax.fori_loop(4 * g, min(4 * g + 4, NZ - 1), one, 0)

    forward(mine)
    yield waiting

    def flip(k, c):
        xt_v[k] = x_v[k].T
        return c

    lax.fori_loop(0, SAMPLES, flip, 0)
    arrived(2)
    yield waiting
    a_v[...] = g1a_v[...].reshape(RANK, RANK) * gt_v[...] * (1.0 / (MIC_ALL * SAMPLES))
    invert(
        a_v,
        {
            0: lambda: forward_group(3),
            2: lambda: forward_group(2),
            4: lambda: forward_group(1),
            6: lambda: forward_group(0),
        },
    )
    yield waiting
    arrived(12)
    yield waiting
    raw = -exact_dot(yall_v[...], a_v[...])
    raw_v[...] = raw

    half = x // 2
    half_lanes = pl.ds(pl.multiple_of(half * 128, 128), 128)
    g2_v[...] = exact_dot(raw_v[:, half_lanes], raw, ((0,), (0,)))
    send_src(
        lambda ss: g2_v.at[eight((x % 2) * NSRC + ss), :],
        g2s_v.at[src],
        g2s_v.at[pl.ds(0, NSRC - 1)],
        13,
    )
    g2s_v[src] = g2_v[eight((x % 2) * NSRC + src), :]

    for b in range(SRC_DEV // SRC_BLK):
        keep = blk_ref[0, b].astype(F32)
        rows = slice(b * SRC_BLK, (b + 1) * SRC_BLK)
        low_v[rows, :] = (raw_v[rows, :] * keep).astype(BF16)

    def mic_part(kk, acc):
        left = xt_v[pl.ds(kk * 8, 8)].reshape(8 * MIC_DEV, SRC_DEV)
        prod = jnp.dot(left, low_v[...], preferred_element_type=F32)
        for i in range(8):
            piece = prod[i * MIC_DEV : (i + 1) * MIC_DEV, :]
            p_v[kk * 8 + i] = piece
            acc = acc + time_ref[pl.ds(kk * 8 + i, 1), :] * piece
        return acc

    mm_v[...] = lax.fori_loop(0, SAMPLES // 8, mic_part, jnp.zeros((MIC_DEV, RANK), F32))

    def sixteen(k):
        return pl.ds(pl.multiple_of(k * 16, 16), 16)

    mic_rows = sixteen(src)
    send_src(
        lambda ss: mm_v.at[sixteen(ss), :], mr_v.at[src], mr_v.at[pl.ds(0, NSRC - 1)], 15
    )
    mr_v[src] = mm_v[mic_rows, :]
    yield waiting
    arrived(13)
    g2p_v[...] = jnp.sum(g2s_v[...], axis=0)
    send_xs(g2p_v, g2a_v, 14)
    arrived(15)
    m16_v[...] = jnp.sum(mr_v[...], axis=0)
    send_xs(m16_v, mall_v, 16)
    arrived(14)
    yield waiting
    gram_src = g2a_v[...].reshape(RANK, RANK)
    src_row, src_col = scales_of(gram_src, SRC_ALL)
    gram_src = gram_src / (src_row * src_col)
    gn_v[...] = gram_src
    a_v[...] = gram_src * gt_v[...] * (1.0 / (SRC_ALL * SAMPLES))
    invert(a_v)
    yield waiting
    arrived(16)
    mraw = -exact_dot(mall_v[...].reshape(NX * MIC_DEV, RANK) / src_row, a_v[...])
    mraw_v[...] = mraw

    g3_v[...] = exact_dot(mraw_v[:, half_lanes], mraw, ((0,), (0,)))
    g3s_v[...] = g3_v[eight((x % 2) * NSRC + src), :]
    send_z(g3s_v, g3z_v, 18)

    mic_own = pl.ds(pl.multiple_of(x * MIC_DEV, MIC_DEV), MIC_DEV)

    def time_part(k, c):
        t_v[k] = jnp.sum(p_v[k] * mraw_v[mic_own, :], axis=0, keepdims=True)
        return c

    lax.fori_loop(0, SAMPLES, time_part, 0)
    expect(20, ts_v.at[pl.ds(0, NXS - 1)])

    def send_sample(d, c):
        q = (p + d) % NXS
        send(t_v.at[q], ts_v.at[p], 20, at(z, q // NSRC, q % NSRC))
        return c

    lax.fori_loop(1, NXS, send_sample, 0)
    ts_v[p] = t_v[p]
    yield waiting

    raw_v[...] = raw_v[...] / src_row
    store_src = pltpu.make_async_copy(raw_v, src_out, load_sem.at[0])
    store_src.start()
    arrived(20)
    tp_v[...] = jnp.sum(ts_v[...], axis=0)
    send_z(tp_v, tz_v, 21)
    arrived(18)
    yield waiting
    g3p_v[...] = jnp.sum(g3z_v[...], axis=0)
    send_xs(g3p_v, g3a_v, 19)
    arrived(21)
    tq_v[...] = jnp.sum(tz_v[...], axis=0)
    send_xs(tq_v, ta_v, 22)
    arrived(19)
    yield waiting

    gram_mic = g3a_v[...].reshape(RANK, RANK)
    mic_row, mic_col = scales_of(gram_mic, MIC_ALL)
    a_v[...] = gn_v[...] * (gram_mic / (mic_row * mic_col)) * (1.0 / (SRC_ALL * MIC_ALL))
    mraw_v[mic_own, :] = mraw_v[mic_own, :] / mic_row
    store_mic = pltpu.make_async_copy(mraw_v.at[mic_own, :], mic_out, load_sem.at[1])
    store_mic.start()
    invert(a_v)
    yield waiting

    arrived(22)
    total = ta_v[...].reshape(SAMPLES, RANK)
    total = total / (src_row * mic_row)
    time_raw = -exact_dot(total, a_v[...])
    time_diag = jnp.sum(time_raw * time_raw, axis=0, keepdims=True)
    time_v[...] = time_raw / jnp.sqrt(time_diag / SAMPLES + 1e-06)
    store_time = pltpu.make_async_copy(time_v, time_out, load_sem.at[2])
    store_time.start()
    store_src.wait()
    store_mic.wait()
    store_time.wait()

    yield waiting


def kernel(*refs, stop=None):
    send_sem, recv_sem = refs[-2:]
    for count, waiting in enumerate(sweep(*refs)):
        if count == stop:
            break
    for stage, (ref, coming) in waiting.items():
        if coming:
            drain(ref, recv_sem.at[stage])
        drain(ref, send_sem.at[stage])


def copy_out(*refs):
    copies = [pltpu.make_async_copy(refs[i], refs[3 + i], refs[6].at[i]) for i in range(3)]
    for copy in copies:
        copy.start()
    for copy in copies:
        copy.wait()


def on_device(tensor_slab, observed_blocks, mic_factor, time_factor, stop=None, collective_id=0, name=None):
    hbm = pl.BlockSpec(memory_space=pltpu.HBM)
    outs = (
        jax.ShapeDtypeStruct((SRC_DEV, RANK), F32),
        jax.ShapeDtypeStruct((MIC_DEV, RANK), F32),
        jax.ShapeDtypeStruct((SAMPLES, RANK), F32),
    )
    results = pl.pallas_call(
        functools.partial(kernel, stop=stop),
        name=name,
        out_shape=outs,
        in_specs=[hbm] * 4,
        out_specs=(hbm,) * 3,
        scratch_shapes=[
            pltpu.SMEM((1, SRC_DEV // SRC_BLK), jnp.int32),
            pltpu.VMEM((MIC_DEV, RANK), F32),
            pltpu.VMEM((SAMPLES, RANK), F32),
            pltpu.VMEM((SAMPLES, SRC_DEV, MIC_DEV), BF16),
            pltpu.VMEM((SAMPLES, MIC_DEV, SRC_DEV), BF16),
            pltpu.VMEM((SAMPLES * MIC_DEV, RANK), BF16),
            pltpu.VMEM((SAMPLES, MIC_DEV, RANK), F32),
            pltpu.VMEM((SRC_DEV, RANK), F32),
            pltpu.VMEM((NX - 1, 128, RANK), F32),
            pltpu.VMEM((128, RANK), F32),
            pltpu.VMEM((NZ, 8, RANK), F32),
            pltpu.VMEM((SRC_DEV, RANK), F32),
            pltpu.VMEM((SRC_DEV, RANK), F32),
            pltpu.VMEM((SRC_DEV, RANK), BF16),
            pltpu.VMEM((RANK, RANK), F32),
            pltpu.VMEM((RANK, RANK), F32),
            pltpu.VMEM((RANK, RANK), F32),
            pltpu.VMEM((RANK, RANK), F32),
            pltpu.VMEM((NX, 8, RANK), F32),
            pltpu.VMEM((8, RANK), F32),
            pltpu.VMEM((NZ, 8, RANK), F32),
            pltpu.VMEM((8, RANK), F32),
            pltpu.VMEM((NXS, 8, RANK), F32),
            pltpu.VMEM((128, RANK), F32),
            pltpu.VMEM((NSRC, 8, RANK), F32),
            pltpu.VMEM((8, RANK), F32),
            pltpu.VMEM((NXS, 8, RANK), F32),
            pltpu.VMEM((MIC_DEV, RANK), F32),
            pltpu.VMEM((NSRC, 16, RANK), F32),
            pltpu.VMEM((16, RANK), F32),
            pltpu.VMEM((NXS, 16, RANK), F32),
            pltpu.VMEM((NX * MIC_DEV, RANK), F32),
            pltpu.VMEM((128, RANK), F32),
            pltpu.VMEM((8, RANK), F32),
            pltpu.VMEM((NZ, 8, RANK), F32),
            pltpu.VMEM((8, RANK), F32),
            pltpu.VMEM((NXS, 8, RANK), F32),
            pltpu.VMEM((NXS, 1, RANK), F32),
            pltpu.VMEM((NXS, 1, RANK), F32),
            pltpu.VMEM((1, RANK), F32),
            pltpu.VMEM((NZ, 1, RANK), F32),
            pltpu.VMEM((1, RANK), F32),
            pltpu.VMEM((NXS, 1, RANK), F32),
            pltpu.VMEM((SAMPLES, RANK), F32),
            pltpu.SemaphoreType.DMA((4,)),
            pltpu.SemaphoreType.DMA((STAGES,)),
            pltpu.SemaphoreType.DMA((STAGES,)),
        ],
        compiler_params=pltpu.CompilerParams(
            collective_id=collective_id, has_side_effects=True, vmem_limit_bytes=60 * 1024 * 1024
        ),
    )(tensor_slab, observed_blocks.reshape(1, SRC_DEV // SRC_BLK), mic_factor, time_factor)
    return pl.pallas_call(
        copy_out,
        out_shape=outs,
        in_specs=[hbm] * 3,
        out_specs=(hbm,) * 3,
        scratch_shapes=[pltpu.SemaphoreType.DMA((3,))],
        compiler_params=pltpu.CompilerParams(vmem_limit_bytes=60 * 1024 * 1024),
    )(*results)


def solution(mesh):
    placed = (P(None, "src", "mic"), P("src", "mic"), P("mic", None), P())
    return jax.shard_map(
        on_device,
        mesh=mesh,
        in_specs=placed,
        out_specs=(P("src", None), P("mic", None), P()),
        check_vma=False,
    )
```

```python
import functools

import jax
import jax.numpy as jnp
from jax import lax
from jax.experimental import pallas as pl
from jax.experimental.pallas import tpu as pltpu
from jax.sharding import PartitionSpec as P

MESH = pl.DeviceIdType.MESH
F32 = jnp.float32
BF16 = jnp.bfloat16

RANK = 256
SAMPLES = 32
SRC_DEV = 512
MIC_DEV = 128
SRC_BLK = 64
NX = 4
NZ = 16
NSRC = 8
NXS = NX * NSRC
SRC_ALL = SRC_DEV * NSRC
MIC_ALL = MIC_DEV * NX * NZ
BLK = 32
STAGES = 23


def exact_dot(a, b, dims=((1,), (0,))):
    return lax.dot_general(
        a, b, (dims, ((), ())), precision=lax.Precision.HIGHEST, preferred_element_type=F32
    )


def split3(a):
    first = a.astype(BF16)
    rest = a - first.astype(F32)
    second = rest.astype(BF16)
    third = (rest - second.astype(F32)).astype(BF16)
    return first, second, third


def outer_dot(a, b):
    a0, a1, a2 = split3(a)
    b0, b1, b2 = split3(b)
    left = jnp.concatenate([a0, a0, a1, a1, a0, a2], axis=0)
    right = jnp.concatenate([b0, b1, b0, b1, b2, b0], axis=0)
    return lax.dot_general(left, right, (((0,), (0,)), ((), ())), preferred_element_type=F32)


def twice(v):
    return jnp.concatenate([v, v], axis=1)


def eliminate(panel, rel, tile, first):
    sub = lax.broadcasted_iota(jnp.int32, (8, RANK), 0)
    sub_tile = lax.broadcasted_iota(jnp.int32, (8, 128), 0)
    groups = BLK // 8
    rows = [panel[8 * g : 8 * g + 8, :] for g in range(groups)]
    z_parts, w_parts = [], []
    for b in range(groups):
        lo = first + 8 * b
        col = {}
        for g in range(b, groups):
            part = rows[g][:, 128 * tile : 128 * tile + 128]
            col[g] = [jnp.broadcast_to(part[:, lo + j : lo + j + 1], (8, 128)) for j in range(8)]
        s = {}
        for k in range(8):
            for l in range(k, 8):
                s[k, l] = jnp.broadcast_to(col[b][l][k : k + 1, :], (8, 128))
        inside = (rel >= 8 * b) & (rel < 8 * b + 8)
        own = jnp.where(inside, jnp.where(rel == sub + 8 * b, -1.0, 0.0), rows[b])
        for g in range(b + 1, groups):
            rows[g] = jnp.where(inside, 0.0, rows[g])
        r = [jnp.broadcast_to(own[k : k + 1, :], (8, RANK)) for k in range(8)]
        inv = [None] * 8
        for j in range(0, 8, 2):
            a, m, d = s[j, j], s[j, j + 1], s[j + 1, j + 1]
            inv_det = 1.0 / (a * d - m * m)
            inv_a = 1.0 / a
            later = range(j + 2, 8)
            x = {l: s[j, l] for l in later}
            y = {l: s[j + 1, l] for l in later}
            u = {l: d * x[l] - m * y[l] for l in later}
            v = {l: a * y[l] - m * x[l] for l in later}
            for k in later:
                for l in range(k, 8):
                    s[k, l] = s[k, l] - (u[k] * x[l] + v[k] * y[l]) * inv_det
            f = m * inv_a
            r[j + 1] = r[j + 1] - twice(f) * r[j]
            inv[j] = inv_a
            inv[j + 1] = a * inv_det
            for k in later:
                r[k] = r[k] - twice(x[k] * inv_a) * r[j] - twice(v[k] * inv_det) * r[j + 1]
            for g in range(b + 1, groups):
                c1 = (col[g][j + 1] - col[g][j] * f) * inv[j + 1]
                c0 = col[g][j] * inv_a
                rows[g] = rows[g] - twice(c0) * r[j] - twice(c1) * r[j + 1]
                for l in later:
                    col[g][l] = col[g][l] - c0 * x[l] - c1 * (v[l] * inv_a)
        z, w = r[0], inv[0]
        for k in range(1, 8):
            z = jnp.where(sub == k, r[k], z)
            w = jnp.where(sub_tile == k, inv[k], w)
        z = jnp.where((rel >= 8 * b + 8) & (rel < BLK), 0.0, z)
        z_parts.append(z)
        w_parts.append(z * twice(w))
    return jnp.concatenate(z_parts, axis=0), jnp.concatenate(w_parts, axis=0)


def invert_block(a_ref, i):
    lane = lax.broadcasted_iota(jnp.int32, (8, RANK), 1)
    lane_row = lax.broadcasted_iota(jnp.int32, (1, RANK), 1)
    base = i * BLK
    rows = slice(base, base + BLK)
    z, w = eliminate(a_ref[rows, :], lane - base, base // 128, base % 128)
    inside = (lane_row >= base) & (lane_row < base + BLK)
    update = outer_dot(z, w)
    a_ref[rows, :] = jnp.zeros((BLK, RANK), F32)
    a_ref[...] = jnp.where(inside, 0.0, a_ref[...]) - update


def invert(a_ref, between=None):
    for i in range(RANK // BLK):
        invert_block(a_ref, i)
        if between is not None and i in between:
            between[i]()


def diagonal(gram):
    rows = lax.broadcasted_iota(jnp.int32, (RANK, RANK), 0)
    cols = lax.broadcasted_iota(jnp.int32, (RANK, RANK), 1)
    only = jnp.where(rows == cols, gram, 0.0)
    return jnp.sum(only, axis=0, keepdims=True), jnp.sum(only, axis=1, keepdims=True)


def scales_of(gram, count):
    row, col = diagonal(gram)
    return jnp.sqrt(row / count + 1e-06), jnp.sqrt(col / count + 1e-06)


def drain(ref, sem):
    pltpu.make_async_copy(ref, ref, sem).wait()


def ring_step(i, size=NZ):
    half = (i + 1) // 2
    return size // 2 + half - 2 * half * (i % 2)


def eight(k):
    return pl.ds(pl.multiple_of(k * 8, 8), 8)


def sweep(
    x_hbm,
    blk_hbm,
    mic_hbm,
    time_hbm,
    src_out,
    mic_out,
    time_out,
    blk_ref,
    mic_ref,
    time_ref,
    x_v,
    xt_v,
    kr_v,
    p_v,
    y_v,
    yx_v,
    y128_v,
    yz_v,
    yall_v,
    raw_v,
    low_v,
    gt_v,
    a_v,
    gn_v,
    g1_v,
    g1x_v,
    g1s_v,
    g1z_v,
    g1p_v,
    g1a_v,
    g2_v,
    g2s_v,
    g2p_v,
    g2a_v,
    mm_v,
    mr_v,
    m16_v,
    mall_v,
    mraw_v,
    g3_v,
    g3s_v,
    g3z_v,
    g3p_v,
    g3a_v,
    t_v,
    ts_v,
    tp_v,
    tz_v,
    tq_v,
    ta_v,
    time_v,
    load_sem,
    send_sem,
    recv_sem,
):
    me_mic = lax.axis_index("mic")
    src = lax.axis_index("src")
    z = me_mic // NX
    x = me_mic % NX
    p = x * NSRC + src

    def at(zz, xx, ss):
        return (zz * NX + xx, ss)

    load_mic = pltpu.make_async_copy(mic_hbm, mic_ref, load_sem.at[0])
    load_time = pltpu.make_async_copy(time_hbm, time_ref, load_sem.at[1])
    load_blk = pltpu.make_async_copy(blk_hbm, blk_ref, load_sem.at[2])
    load = pltpu.make_async_copy(x_hbm, x_v, load_sem.at[3])
    load_mic.start()
    load_time.start()
    load_blk.start()
    load.start()

    barrier = pltpu.get_barrier_semaphore()

    def greet_z(i, c):
        zz = (z + ring_step(i)) % NZ
        pl.semaphore_signal(barrier, inc=1, device_id=at(zz, x, src), device_id_type=MESH)
        return c

    def greet_xs(d, c):
        q = (p + d) % NXS
        pl.semaphore_signal(
            barrier, inc=1, device_id=at(z, q // NSRC, q % NSRC), device_id_type=MESH
        )
        return c

    lax.fori_loop(0, NZ - 1, greet_z, 0)
    lax.fori_loop(1, NXS, greet_xs, 0)

    waiting = {}

    def expect(stage, ref):
        waiting[stage] = [ref, True]

    def arrived(stage):
        drain(waiting[stage][0], recv_sem.at[stage])
        waiting[stage][1] = False

    def send(src_ref, dst_ref, stage, device):
        pltpu.make_async_remote_copy(
            src_ref=src_ref,
            dst_ref=dst_ref,
            send_sem=send_sem.at[stage],
            recv_sem=recv_sem.at[stage],
            device_id=device,
            device_id_type=MESH,
        ).start()

    def send_x(gram_ref, dst, stage):
        expect(stage, dst.at[pl.ds(0, NX - 1)])

        def one(d, c):
            xx = (x + d) % NX
            send(gram_ref.at[eight(xx * NSRC + src), :], dst.at[x], stage, at(z, xx, src))
            return c

        lax.fori_loop(1, NX, one, 0)
        dst[x] = gram_ref[eight(p), :]

    def send_z(piece_ref, dst, stage):
        expect(stage, dst.at[pl.ds(0, NZ - 1)])

        def one(i, c):
            send(piece_ref, dst.at[z], stage, at((z + ring_step(i)) % NZ, x, src))
            return c

        lax.fori_loop(0, NZ - 1, one, 0)
        dst[z] = piece_ref[...]

    def plane_step(i):
        xx = (x + ring_step(i // NSRC, NX)) % NX
        yy = (src // 2 + ring_step(i // 2 % (NSRC // 2), NSRC // 2)) % (NSRC // 2)
        return xx, yy * 2 + (src % 2 + 1 + i) % 2

    def send_xs(piece_ref, dst, stage):
        expect(stage, dst.at[pl.ds(0, NXS - 1)])

        def one(i, c):
            xx, ss = plane_step(i)
            send(piece_ref, dst.at[p], stage, at(z, xx, ss))
            return c

        lax.fori_loop(0, NXS - 1, one, 0)
        dst[p] = piece_ref[...]

    def send_src(piece_of, dst_ref, expected, stage):
        expect(stage, expected)

        def one(i, c):
            ss = plane_step(NXS - NSRC + i)[1]
            send(piece_of(ss), dst_ref, stage, at(z, x, ss))
            return c

        lax.fori_loop(0, NSRC - 1, one, 0)

    load_mic.wait()
    load_time.wait()
    mic = mic_ref[...]
    g1_v[...] = exact_dot(mic, mic, ((0,), (0,)))
    times = time_ref[...]
    gt_v[...] = exact_dot(times, times, ((0,), (0,)))
    mic_low = mic.astype(BF16).astype(F32)

    def make_kr(k, c):
        kr_v[pl.ds(pl.multiple_of(k * MIC_DEV, MIC_DEV), MIC_DEV), :] = (
            time_ref[pl.ds(k, 1), :] * mic_low
        ).astype(BF16)
        return c

    lax.fori_loop(0, SAMPLES, make_kr, 0)

    load_blk.wait()
    load.wait()
    for xx in range(NX):
        left = jnp.concatenate(
            [x_v[k, xx * 128 : (xx + 1) * 128, :] for k in range(SAMPLES)], axis=1
        )
        part = jnp.dot(left, kr_v[...], preferred_element_type=F32)
        for h in range(2):
            keep = blk_ref[0, xx * 2 + h].astype(F32)
            rows = slice(xx * 128 + h * 64, xx * 128 + (h + 1) * 64)
            y_v[rows, :] = part[h * 64 : (h + 1) * 64, :] * keep

    pl.semaphore_wait(barrier, NZ - 1 + NXS - 1)
    yield waiting

    send_x(g1_v, g1x_v, 0)

    for g in range(4):
        expect(3 + g, yx_v.at[0, pl.ds(0, 96), :])

        def row_group(ix, c, g=g):
            dx = ring_step(ix, NX)
            xx = (x + dx) % NX

            def one(i, c):
                zz = (z + ring_step(i)) % NZ
                send(
                    y_v.at[eight(xx * NZ + zz), :],
                    yx_v.at[dx - 1, eight(zz), :],
                    3 + g,
                    at(z, xx, src),
                )
                return c

            return lax.fori_loop(4 * g, 4 * g + 4, one, c)

        lax.fori_loop(0, NX - 1, row_group, 0)

    arrived(0)
    g1s_v[...] = (g1x_v[0] + g1x_v[1]) + (g1x_v[2] + g1x_v[3])
    send_z(g1s_v, g1z_v, 1)

    expect(7, yz_v.at[pl.ds(0, NZ - 1)])
    for g in range(4):
        arrived(3 + g)

        def sum_send(i, c):
            zz = (z + ring_step(i)) % NZ
            rows = eight(zz)
            y128_v[rows, :] = (y_v[eight(x * NZ + zz), :] + yx_v[0, rows, :]) + (
                yx_v[1, rows, :] + yx_v[2, rows, :]
            )
            send(y128_v.at[rows, :], yz_v.at[i], 7, at(zz, x, src))
            return c

        lax.fori_loop(4 * g, min(4 * g + 4, NZ - 1), sum_send, 0)
    own = eight(z)
    yz_v[NZ - 1] = (y_v[eight(x * NZ + z), :] + yx_v[0, own, :]) + (
        yx_v[1, own, :] + yx_v[2, own, :]
    )
    yield waiting

    def flip(k, c):
        xt_v[k] = x_v[k].T
        return c

    lax.fori_loop(0, SAMPLES, flip, 0)

    arrived(1)
    g1p_v[...] = jnp.sum(g1z_v[...], axis=0)
    send_xs(g1p_v, g1a_v, 2)

    arrived(7)
    mine = eight(x * NZ + z)
    yall_v[mine, :] = jnp.sum(yz_v[...], axis=0)
    for g in range(4):
        last = min(4 * g + 4, NZ - 1)
        expect(8 + g, yall_v.at[pl.ds(0, 8 * (last - 4 * g)), :])

        def back_z(i, c, g=g):
            zz = (z + ring_step(i)) % NZ
            send(yall_v.at[mine, :], yall_v.at[mine, :], 8 + g, at(zz, x, src))
            return c

        lax.fori_loop(4 * g, last, back_z, 0)

    expect(12, yall_v.at[pl.ds(0, 128 * (NX - 1)), :])

    def forward(rows):
        def one(ix, c):
            xx = (x + ring_step(ix, NX)) % NX
            send(yall_v.at[rows, :], yall_v.at[rows, :], 12, at(z, xx, src))
            return c

        lax.fori_loop(0, NX - 1, one, 0)

    def forward_group(g):
        arrived(8 + g)

        def one(i, c):
            forward(eight(x * NZ + (z + NZ - ring_step(i)) % NZ))
            return c

        lax.fori_loop(4 * g, min(4 * g + 4, NZ - 1), one, 0)

    forward(mine)
    yield waiting

    forward_group(3)
    forward_group(2)
    arrived(2)
    yield waiting
    a_v[...] = g1a_v[...].reshape(RANK, RANK) * gt_v[...] * (1.0 / (MIC_ALL * SAMPLES))
    invert(a_v, {1: lambda: forward_group(1), 3: lambda: forward_group(0)})
    yield waiting
    arrived(12)
    yield waiting
    raw = -exact_dot(yall_v[...], a_v[...])
    raw_v[...] = raw

    half = x // 2
    half_lanes = pl.ds(pl.multiple_of(half * 128, 128), 128)
    g2_v[...] = exact_dot(raw_v[:, half_lanes], raw, ((0,), (0,)))
    send_src(
        lambda ss: g2_v.at[eight((x % 2) * NSRC + ss), :],
        g2s_v.at[src],
        g2s_v.at[pl.ds(0, NSRC - 1)],
        13,
    )
    g2s_v[src] = g2_v[eight((x % 2) * NSRC + src), :]

    for b in range(SRC_DEV // SRC_BLK):
        keep = blk_ref[0, b].astype(F32)
        rows = slice(b * SRC_BLK, (b + 1) * SRC_BLK)
        low_v[rows, :] = (raw_v[rows, :] * keep).astype(BF16)

    def mic_part(kk, acc):
        left = xt_v[pl.ds(kk * 8, 8)].reshape(8 * MIC_DEV, SRC_DEV)
        prod = jnp.dot(left, low_v[...], preferred_element_type=F32)
        for i in range(8):
            piece = prod[i * MIC_DEV : (i + 1) * MIC_DEV, :]
            p_v[kk * 8 + i] = piece
            acc = acc + time_ref[pl.ds(kk * 8 + i, 1), :] * piece
        return acc

    mm_v[...] = lax.fori_loop(0, SAMPLES // 8, mic_part, jnp.zeros((MIC_DEV, RANK), F32))

    def sixteen(k):
        return pl.ds(pl.multiple_of(k * 16, 16), 16)

    mic_rows = sixteen(src)
    send_src(
        lambda ss: mm_v.at[sixteen(ss), :], mr_v.at[src], mr_v.at[pl.ds(0, NSRC - 1)], 15
    )
    mr_v[src] = mm_v[mic_rows, :]
    yield waiting
    arrived(13)
    g2p_v[...] = jnp.sum(g2s_v[...], axis=0)
    send_xs(g2p_v, g2a_v, 14)
    arrived(15)
    m16_v[...] = jnp.sum(mr_v[...], axis=0)
    send_xs(m16_v, mall_v, 16)
    arrived(14)
    yield waiting
    gram_src = g2a_v[...].reshape(RANK, RANK)
    src_row, src_col = scales_of(gram_src, SRC_ALL)
    gram_src = gram_src / (src_row * src_col)
    gn_v[...] = gram_src
    a_v[...] = gram_src * gt_v[...] * (1.0 / (SRC_ALL * SAMPLES))
    invert(a_v)
    yield waiting
    arrived(16)
    mraw = -exact_dot(mall_v[...].reshape(NX * MIC_DEV, RANK) / src_row, a_v[...])
    mraw_v[...] = mraw

    g3_v[...] = exact_dot(mraw_v[:, half_lanes], mraw, ((0,), (0,)))
    g3s_v[...] = g3_v[eight((x % 2) * NSRC + src), :]
    send_z(g3s_v, g3z_v, 18)

    mic_own = pl.ds(pl.multiple_of(x * MIC_DEV, MIC_DEV), MIC_DEV)

    def time_part(k, c):
        t_v[k] = jnp.sum(p_v[k] * mraw_v[mic_own, :], axis=0, keepdims=True)
        return c

    lax.fori_loop(0, SAMPLES, time_part, 0)
    expect(20, ts_v.at[pl.ds(0, NXS - 1)])

    def send_sample(i, c):
        xx, ss = plane_step(i)
        send(t_v.at[xx * NSRC + ss], ts_v.at[p], 20, at(z, xx, ss))
        return c

    lax.fori_loop(0, NXS - 1, send_sample, 0)
    ts_v[p] = t_v[p]
    yield waiting

    raw_v[...] = raw_v[...] / src_row
    store_src = pltpu.make_async_copy(raw_v, src_out, load_sem.at[0])
    store_src.start()
    arrived(20)
    tp_v[...] = jnp.sum(ts_v[...], axis=0)
    send_z(tp_v, tz_v, 21)
    arrived(18)
    yield waiting
    g3p_v[...] = jnp.sum(g3z_v[...], axis=0)
    send_xs(g3p_v, g3a_v, 19)
    arrived(21)
    tq_v[...] = jnp.sum(tz_v[...], axis=0)
    send_xs(tq_v, ta_v, 22)
    arrived(19)
    yield waiting

    gram_mic = g3a_v[...].reshape(RANK, RANK)
    mic_row, mic_col = scales_of(gram_mic, MIC_ALL)
    a_v[...] = gn_v[...] * (gram_mic / (mic_row * mic_col)) * (1.0 / (SRC_ALL * MIC_ALL))
    mraw_v[mic_own, :] = mraw_v[mic_own, :] / mic_row
    store_mic = pltpu.make_async_copy(mraw_v.at[mic_own, :], mic_out, load_sem.at[1])
    store_mic.start()
    invert(a_v)
    yield waiting

    arrived(22)
    total = ta_v[...].reshape(SAMPLES, RANK)
    total = total / (src_row * mic_row)
    time_raw = -exact_dot(total, a_v[...])
    time_diag = jnp.sum(time_raw * time_raw, axis=0, keepdims=True)
    time_v[...] = time_raw / jnp.sqrt(time_diag / SAMPLES + 1e-06)
    store_time = pltpu.make_async_copy(time_v, time_out, load_sem.at[2])
    store_time.start()
    store_src.wait()
    store_mic.wait()
    store_time.wait()

    yield waiting


def kernel(*refs, stop=None):
    send_sem, recv_sem = refs[-2:]
    for count, waiting in enumerate(sweep(*refs)):
        if count == stop:
            break
    for stage, (ref, coming) in waiting.items():
        if coming:
            drain(ref, recv_sem.at[stage])
        drain(ref, send_sem.at[stage])


def copy_out(src_in, mic_in, time_in, src_out, mic_out, time_out):
    src_out[...] = src_in[...]
    mic_out[...] = mic_in[...]
    time_out[...] = time_in[...]


def on_device(tensor_slab, observed_blocks, mic_factor, time_factor, stop=None, collective_id=0, name=None):
    hbm = pl.BlockSpec(memory_space=pltpu.HBM)
    outs = (
        jax.ShapeDtypeStruct((SRC_DEV, RANK), F32),
        jax.ShapeDtypeStruct((MIC_DEV, RANK), F32),
        jax.ShapeDtypeStruct((SAMPLES, RANK), F32),
    )
    results = pl.pallas_call(
        functools.partial(kernel, stop=stop),
        name=name,
        out_shape=outs,
        in_specs=[hbm] * 4,
        out_specs=(hbm,) * 3,
        scratch_shapes=[
            pltpu.SMEM((1, SRC_DEV // SRC_BLK), jnp.int32),
            pltpu.VMEM((MIC_DEV, RANK), F32),
            pltpu.VMEM((SAMPLES, RANK), F32),
            pltpu.VMEM((SAMPLES, SRC_DEV, MIC_DEV), BF16),
            pltpu.VMEM((SAMPLES, MIC_DEV, SRC_DEV), BF16),
            pltpu.VMEM((SAMPLES * MIC_DEV, RANK), BF16),
            pltpu.VMEM((SAMPLES, MIC_DEV, RANK), F32),
            pltpu.VMEM((SRC_DEV, RANK), F32),
            pltpu.VMEM((NX - 1, 128, RANK), F32),
            pltpu.VMEM((128, RANK), F32),
            pltpu.VMEM((NZ, 8, RANK), F32),
            pltpu.VMEM((SRC_DEV, RANK), F32),
            pltpu.VMEM((SRC_DEV, RANK), F32),
            pltpu.VMEM((SRC_DEV, RANK), BF16),
            pltpu.VMEM((RANK, RANK), F32),
            pltpu.VMEM((RANK, RANK), F32),
            pltpu.VMEM((RANK, RANK), F32),
            pltpu.VMEM((RANK, RANK), F32),
            pltpu.VMEM((NX, 8, RANK), F32),
            pltpu.VMEM((8, RANK), F32),
            pltpu.VMEM((NZ, 8, RANK), F32),
            pltpu.VMEM((8, RANK), F32),
            pltpu.VMEM((NXS, 8, RANK), F32),
            pltpu.VMEM((128, RANK), F32),
            pltpu.VMEM((NSRC, 8, RANK), F32),
            pltpu.VMEM((8, RANK), F32),
            pltpu.VMEM((NXS, 8, RANK), F32),
            pltpu.VMEM((MIC_DEV, RANK), F32),
            pltpu.VMEM((NSRC, 16, RANK), F32),
            pltpu.VMEM((16, RANK), F32),
            pltpu.VMEM((NXS, 16, RANK), F32),
            pltpu.VMEM((NX * MIC_DEV, RANK), F32),
            pltpu.VMEM((128, RANK), F32),
            pltpu.VMEM((8, RANK), F32),
            pltpu.VMEM((NZ, 8, RANK), F32),
            pltpu.VMEM((8, RANK), F32),
            pltpu.VMEM((NXS, 8, RANK), F32),
            pltpu.VMEM((NXS, 1, RANK), F32),
            pltpu.VMEM((NXS, 1, RANK), F32),
            pltpu.VMEM((1, RANK), F32),
            pltpu.VMEM((NZ, 1, RANK), F32),
            pltpu.VMEM((1, RANK), F32),
            pltpu.VMEM((NXS, 1, RANK), F32),
            pltpu.VMEM((SAMPLES, RANK), F32),
            pltpu.SemaphoreType.DMA((4,)),
            pltpu.SemaphoreType.DMA((STAGES,)),
            pltpu.SemaphoreType.DMA((STAGES,)),
        ],
        compiler_params=pltpu.CompilerParams(
            collective_id=collective_id, has_side_effects=True, vmem_limit_bytes=60 * 1024 * 1024
        ),
    )(tensor_slab, observed_blocks.reshape(1, SRC_DEV // SRC_BLK), mic_factor, time_factor)
    vmem = pl.BlockSpec(memory_space=pltpu.VMEM)
    return pl.pallas_call(
        copy_out,
        out_shape=outs,
        in_specs=[vmem] * 3,
        out_specs=(vmem,) * 3,
        compiler_params=pltpu.CompilerParams(vmem_limit_bytes=60 * 1024 * 1024),
    )(*results)


def solution(mesh):
    placed = (P(None, "src", "mic"), P("src", "mic"), P("mic", None), P())
    return jax.shard_map(
        on_device,
        mesh=mesh,
        in_specs=placed,
        out_specs=(P("src", None), P("mic", None), P()),
        check_vma=False,
    )
```

```python
import functools

import jax
import jax.numpy as jnp
from jax import lax
from jax.experimental import pallas as pl
from jax.experimental.pallas import tpu as pltpu
from jax.sharding import PartitionSpec as P

MESH = pl.DeviceIdType.MESH
F32 = jnp.float32
BF16 = jnp.bfloat16

RANK = 256
SAMPLES = 32
SRC_DEV = 512
MIC_DEV = 128
SRC_BLK = 64
NX = 4
NZ = 16
NSRC = 8
NXS = NX * NSRC
SRC_ALL = SRC_DEV * NSRC
MIC_ALL = MIC_DEV * NX * NZ
BLK = 32
STAGES = 27


def exact_dot(a, b, dims=((1,), (0,))):
    return lax.dot_general(
        a, b, (dims, ((), ())), precision=lax.Precision.HIGHEST, preferred_element_type=F32
    )


def split3(a):
    first = a.astype(BF16)
    rest = a - first.astype(F32)
    second = rest.astype(BF16)
    third = (rest - second.astype(F32)).astype(BF16)
    return first, second, third


def outer_dot(a, b):
    a0, a1, a2 = split3(a)
    b0, b1, b2 = split3(b)
    left = jnp.concatenate([a0, a0, a1, a1, a0, a2], axis=0)
    right = jnp.concatenate([b0, b1, b0, b1, b2, b0], axis=0)
    return lax.dot_general(left, right, (((0,), (0,)), ((), ())), preferred_element_type=F32)


def twice(v):
    return jnp.concatenate([v, v], axis=1)


def eliminate(panel, rel, tile, first):
    sub = lax.broadcasted_iota(jnp.int32, (8, RANK), 0)
    sub_tile = lax.broadcasted_iota(jnp.int32, (8, 128), 0)
    groups = BLK // 8
    rows = [panel[8 * g : 8 * g + 8, :] for g in range(groups)]
    z_parts, w_parts = [], []
    for b in range(groups):
        lo = first + 8 * b
        col = {}
        for g in range(b, groups):
            part = rows[g][:, 128 * tile : 128 * tile + 128]
            col[g] = [jnp.broadcast_to(part[:, lo + j : lo + j + 1], (8, 128)) for j in range(8)]
        s = {}
        for k in range(8):
            for l in range(k, 8):
                s[k, l] = jnp.broadcast_to(col[b][l][k : k + 1, :], (8, 128))
        inside = (rel >= 8 * b) & (rel < 8 * b + 8)
        own = jnp.where(inside, jnp.where(rel == sub + 8 * b, -1.0, 0.0), rows[b])
        for g in range(b + 1, groups):
            rows[g] = jnp.where(inside, 0.0, rows[g])
        r = [jnp.broadcast_to(own[k : k + 1, :], (8, RANK)) for k in range(8)]
        inv = [None] * 8
        for j in range(0, 8, 2):
            a, m, d = s[j, j], s[j, j + 1], s[j + 1, j + 1]
            inv_det = 1.0 / (a * d - m * m)
            inv_a = 1.0 / a
            later = range(j + 2, 8)
            x = {l: s[j, l] for l in later}
            y = {l: s[j + 1, l] for l in later}
            u = {l: d * x[l] - m * y[l] for l in later}
            v = {l: a * y[l] - m * x[l] for l in later}
            for k in later:
                for l in range(k, 8):
                    s[k, l] = s[k, l] - (u[k] * x[l] + v[k] * y[l]) * inv_det
            f = m * inv_a
            r[j + 1] = r[j + 1] - twice(f) * r[j]
            inv[j] = inv_a
            inv[j + 1] = a * inv_det
            for k in later:
                r[k] = r[k] - twice(x[k] * inv_a) * r[j] - twice(v[k] * inv_det) * r[j + 1]
            for g in range(b + 1, groups):
                c1 = (col[g][j + 1] - col[g][j] * f) * inv[j + 1]
                c0 = col[g][j] * inv_a
                rows[g] = rows[g] - twice(c0) * r[j] - twice(c1) * r[j + 1]
                for l in later:
                    col[g][l] = col[g][l] - c0 * x[l] - c1 * (v[l] * inv_a)
        z, w = r[0], inv[0]
        for k in range(1, 8):
            z = jnp.where(sub == k, r[k], z)
            w = jnp.where(sub_tile == k, inv[k], w)
        z = jnp.where((rel >= 8 * b + 8) & (rel < BLK), 0.0, z)
        z_parts.append(z)
        w_parts.append(z * twice(w))
    return jnp.concatenate(z_parts, axis=0), jnp.concatenate(w_parts, axis=0)


def invert_block(a_ref, i):
    lane = lax.broadcasted_iota(jnp.int32, (8, RANK), 1)
    lane_row = lax.broadcasted_iota(jnp.int32, (1, RANK), 1)
    base = i * BLK
    rows = slice(base, base + BLK)
    z, w = eliminate(a_ref[rows, :], lane - base, base // 128, base % 128)
    inside = (lane_row >= base) & (lane_row < base + BLK)
    update = outer_dot(z, w)
    a_ref[rows, :] = jnp.zeros((BLK, RANK), F32)
    a_ref[...] = jnp.where(inside, 0.0, a_ref[...]) - update


def invert(a_ref, between=None):
    for i in range(RANK // BLK):
        invert_block(a_ref, i)
        if between is not None and i in between:
            between[i]()


def diagonal(gram):
    rows = lax.broadcasted_iota(jnp.int32, (RANK, RANK), 0)
    cols = lax.broadcasted_iota(jnp.int32, (RANK, RANK), 1)
    only = jnp.where(rows == cols, gram, 0.0)
    return jnp.sum(only, axis=0, keepdims=True), jnp.sum(only, axis=1, keepdims=True)


def scales_of(gram, count):
    row, col = diagonal(gram)
    return jnp.sqrt(row / count + 1e-06), jnp.sqrt(col / count + 1e-06)


def drain(ref, sem):
    pltpu.make_async_copy(ref, ref, sem).wait()


def ring_step(i, size=NZ):
    half = (i + 1) // 2
    return size // 2 + half - 2 * half * (i % 2)


def eight(k):
    return pl.ds(pl.multiple_of(k * 8, 8), 8)


def sweep(
    x_hbm,
    blk_hbm,
    mic_hbm,
    time_hbm,
    src_out,
    mic_out,
    time_out,
    blk_ref,
    mic_ref,
    time_ref,
    x_v,
    xt_v,
    kr_v,
    p_v,
    y_v,
    yx_v,
    y128_v,
    yz_v,
    yall_v,
    raw_v,
    low_v,
    gt_v,
    a_v,
    gn_v,
    g1_v,
    g1x_v,
    g1s_v,
    c1_v,
    d1_v,
    c1z_v,
    d1z_v,
    c1s_v,
    d1s_v,
    c1a_v,
    d1a_v,
    g2_v,
    g2s_v,
    g2p_v,
    g2a_v,
    mm_v,
    mr_v,
    m16_v,
    mall_v,
    mraw_v,
    g3_v,
    g3s_v,
    c3_v,
    d3_v,
    c3z_v,
    d3z_v,
    c3s_v,
    d3s_v,
    c3a_v,
    d3a_v,
    t_v,
    ts_v,
    tp_v,
    tz_v,
    tq_v,
    ta_v,
    time_v,
    load_sem,
    send_sem,
    recv_sem,
):
    me_mic = lax.axis_index("mic")
    src = lax.axis_index("src")
    z = me_mic // NX
    x = me_mic % NX
    p = x * NSRC + src
    core = src % 2
    q = p // 2

    def at(zz, xx, ss):
        return (zz * NX + xx, ss)

    load_mic = pltpu.make_async_copy(mic_hbm, mic_ref, load_sem.at[0])
    load_time = pltpu.make_async_copy(time_hbm, time_ref, load_sem.at[1])
    load_blk = pltpu.make_async_copy(blk_hbm, blk_ref, load_sem.at[2])
    load = pltpu.make_async_copy(x_hbm, x_v, load_sem.at[3])
    load_mic.start()
    load_time.start()
    load_blk.start()
    load.start()

    barrier = pltpu.get_barrier_semaphore()

    def greet_z(i, c):
        zz = (z + ring_step(i)) % NZ
        pl.semaphore_signal(barrier, inc=1, device_id=at(zz, x, src), device_id_type=MESH)
        return c

    def greet_xs(d, c):
        q = (p + d) % NXS
        pl.semaphore_signal(
            barrier, inc=1, device_id=at(z, q // NSRC, q % NSRC), device_id_type=MESH
        )
        return c

    lax.fori_loop(0, NZ - 1, greet_z, 0)
    lax.fori_loop(1, NXS, greet_xs, 0)

    waiting = {}

    def expect(stage, ref):
        waiting[stage] = [lambda sem: drain(ref, sem), lambda sem: drain(ref, sem), True]

    def expect_by_core(stage, received, sent):
        def by_core(refs):
            def wait(sem):
                for which in range(2):
                    if refs[which] is not None:
                        pl.when(core == which)(functools.partial(drain, refs[which], sem))

            return wait

        waiting[stage] = [by_core(received), by_core(sent), True]

    def arrived(stage):
        waiting[stage][0](recv_sem.at[stage])
        waiting[stage][2] = False

    def send(src_ref, dst_ref, stage, device):
        pltpu.make_async_remote_copy(
            src_ref=src_ref,
            dst_ref=dst_ref,
            send_sem=send_sem.at[stage],
            recv_sem=recv_sem.at[stage],
            device_id=device,
            device_id_type=MESH,
        ).start()

    def send_x(gram_ref, dst, stage):
        expect(stage, dst.at[pl.ds(0, NX - 1)])

        def one(i, c):
            xx = (x + ring_step(i, NX)) % NX
            rows = eight(core * 16 + (xx * NSRC + src) // 2)
            send(gram_ref.at[rows, :], dst.at[x], stage, at(z, xx, src))
            return c

        lax.fori_loop(0, NX - 1, one, 0)
        dst[x] = gram_ref[eight(core * 16 + q), :]

    def send_z(piece_ref, dst, stage):
        expect(stage, dst.at[pl.ds(0, NZ - 1)])

        def one(i, c):
            send(piece_ref, dst.at[z], stage, at((z + ring_step(i)) % NZ, x, src))
            return c

        lax.fori_loop(0, NZ - 1, one, 0)
        dst[z] = piece_ref[...]

    def plane_step(i):
        xx = (x + ring_step(i // NSRC, NX)) % NX
        yy = (src // 2 + ring_step(i // 2 % (NSRC // 2), NSRC // 2)) % (NSRC // 2)
        return xx, yy * 2 + (src % 2 + 1 + i) % 2

    def send_xs(piece_ref, dst, stage):
        expect(stage, dst.at[pl.ds(0, NXS - 1)])

        def one(i, c):
            xx, ss = plane_step(i)
            send(piece_ref, dst.at[p], stage, at(z, xx, ss))
            return c

        lax.fori_loop(0, NXS - 1, one, 0)
        dst[p] = piece_ref[...]

    core_lanes = pl.ds(pl.multiple_of(core * 128, 128), 128)

    def corner_z(piece_ref, one_v, two_v, one_z, two_z, stage):
        one_v[...] = piece_ref[:, core_lanes]
        send_z(one_v, one_z, stage)
        half = two_z.at[pl.ds(0, NZ - 1)]

        @pl.when(core == 0)
        def _():
            two_v[...] = piece_ref[:, 128:]
            send_z(two_v, two_z, stage + 1)

        expect_by_core(stage + 1, (half, None), (half, None))

    def corner_sum(one_v, two_v, one_z, two_z, stage):
        arrived(stage)
        one_v[...] = jnp.sum(one_z[...], axis=0)
        arrived(stage + 1)

        @pl.when(core == 0)
        def _():
            two_v[...] = jnp.sum(two_z[...], axis=0)

    def corner_xs(one_v, two_v, one_a, two_a, stage):
        send_xs(one_v, one_a, stage)

        @pl.when(core == 0)
        def _():
            def one(i, c):
                xx, ss = plane_step(i)
                send(two_v, two_a.at[q], stage + 1, at(z, xx, ss))
                return c

            lax.fori_loop(0, NXS - 1, one, 0)
            two_a[q] = two_v[...]

        expect_by_core(
            stage + 1,
            (two_a.at[pl.ds(0, NXS // 2 - 1)], two_a),
            (one_a.at[pl.ds(0, NXS - 1)], None),
        )

    def corner_gram(one_a, two_a, stage):
        arrived(stage)
        arrived(stage + 1)
        ones = one_a[...].reshape(NXS // 2, 2, 8, 128)
        upper = two_a[...].reshape(128, 128)
        return jnp.concatenate(
            [
                jnp.concatenate([ones[:, 0].reshape(128, 128), upper], axis=1),
                jnp.concatenate([upper.T, ones[:, 1].reshape(128, 128)], axis=1),
            ],
            axis=0,
        )

    def send_src(piece_of, dst_ref, expected, stage):
        expect(stage, expected)

        def one(i, c):
            ss = plane_step(NXS - NSRC + i)[1]
            send(piece_of(ss), dst_ref, stage, at(z, x, ss))
            return c

        lax.fori_loop(0, NSRC - 1, one, 0)

    load_mic.wait()
    load_time.wait()
    mic = mic_ref[...]
    g1_v[...] = exact_dot(mic, mic, ((0,), (0,)))
    times = time_ref[...]
    gt_v[...] = exact_dot(times, times, ((0,), (0,)))
    mic_low = mic.astype(BF16).astype(F32)

    def make_kr(k, c):
        kr_v[pl.ds(pl.multiple_of(k * MIC_DEV, MIC_DEV), MIC_DEV), :] = (
            time_ref[pl.ds(k, 1), :] * mic_low
        ).astype(BF16)
        return c

    lax.fori_loop(0, SAMPLES, make_kr, 0)

    load_blk.wait()
    load.wait()
    for xx in range(NX):
        left = jnp.concatenate(
            [x_v[k, xx * 128 : (xx + 1) * 128, :] for k in range(SAMPLES)], axis=1
        )
        part = jnp.dot(left, kr_v[...], preferred_element_type=F32)
        for h in range(2):
            keep = blk_ref[0, xx * 2 + h].astype(F32)
            rows = slice(xx * 128 + h * 64, xx * 128 + (h + 1) * 64)
            y_v[rows, :] = part[h * 64 : (h + 1) * 64, :] * keep

    pl.semaphore_wait(barrier, NZ - 1 + NXS - 1)
    yield waiting

    send_x(g1_v, g1x_v, 0)

    for g in range(4):
        expect(3 + g, yx_v.at[0, pl.ds(0, 96), :])

        def row_group(ix, c, g=g):
            dx = ring_step(ix, NX)
            xx = (x + dx) % NX

            def one(i, c):
                zz = (z + ring_step(i)) % NZ
                send(
                    y_v.at[eight(xx * NZ + zz), :],
                    yx_v.at[dx - 1, eight(zz), :],
                    3 + g,
                    at(z, xx, src),
                )
                return c

            return lax.fori_loop(4 * g, 4 * g + 4, one, c)

        lax.fori_loop(0, NX - 1, row_group, 0)

    arrived(0)
    g1s_v[...] = (g1x_v[0] + g1x_v[1]) + (g1x_v[2] + g1x_v[3])
    corner_z(g1s_v, c1_v, d1_v, c1z_v, d1z_v, 23)

    expect(7, yz_v.at[pl.ds(0, NZ - 1)])
    for g in range(4):
        arrived(3 + g)

        def sum_send(i, c):
            zz = (z + ring_step(i)) % NZ
            rows = eight(zz)
            y128_v[rows, :] = (y_v[eight(x * NZ + zz), :] + yx_v[0, rows, :]) + (
                yx_v[1, rows, :] + yx_v[2, rows, :]
            )
            send(y128_v.at[rows, :], yz_v.at[i], 7, at(zz, x, src))
            return c

        lax.fori_loop(4 * g, min(4 * g + 4, NZ - 1), sum_send, 0)
    own = eight(z)
    yz_v[NZ - 1] = (y_v[eight(x * NZ + z), :] + yx_v[0, own, :]) + (
        yx_v[1, own, :] + yx_v[2, own, :]
    )
    yield waiting

    def flip(k, c):
        xt_v[k] = x_v[k].T
        return c

    lax.fori_loop(0, SAMPLES, flip, 0)

    corner_sum(c1s_v, d1s_v, c1z_v, d1z_v, 23)
    corner_xs(c1s_v, d1s_v, c1a_v, d1a_v, 1)

    arrived(7)
    mine = eight(x * NZ + z)
    yall_v[mine, :] = jnp.sum(yz_v[...], axis=0)
    for g in range(4):
        last = min(4 * g + 4, NZ - 1)
        expect(8 + g, yall_v.at[pl.ds(0, 8 * (last - 4 * g)), :])

        def back_z(i, c, g=g):
            zz = (z + ring_step(i)) % NZ
            send(yall_v.at[mine, :], yall_v.at[mine, :], 8 + g, at(zz, x, src))
            return c

        lax.fori_loop(4 * g, last, back_z, 0)

    expect(12, yall_v.at[pl.ds(0, 128 * (NX - 1)), :])

    def forward(rows):
        def one(ix, c):
            xx = (x + ring_step(ix, NX)) % NX
            send(yall_v.at[rows, :], yall_v.at[rows, :], 12, at(z, xx, src))
            return c

        lax.fori_loop(0, NX - 1, one, 0)

    def forward_group(g):
        arrived(8 + g)

        def one(i, c):
            forward(eight(x * NZ + (z + NZ - ring_step(i)) % NZ))
            return c

        lax.fori_loop(4 * g, min(4 * g + 4, NZ - 1), one, 0)

    forward(mine)
    yield waiting

    forward_group(3)
    forward_group(2)
    gram_mic = corner_gram(c1a_v, d1a_v, 1)
    yield waiting
    a_v[...] = gram_mic * gt_v[...] * (1.0 / (MIC_ALL * SAMPLES))
    invert(a_v, {1: lambda: forward_group(1), 3: lambda: forward_group(0)})
    yield waiting
    arrived(12)
    yield waiting
    raw = -exact_dot(yall_v[...], a_v[...])
    raw_v[...] = raw

    half = x // 2
    half_lanes = pl.ds(pl.multiple_of(half * 128, 128), 128)
    g2_v[...] = exact_dot(raw_v[:, half_lanes], raw, ((0,), (0,)))
    send_src(
        lambda ss: g2_v.at[eight((x % 2) * NSRC + ss), :],
        g2s_v.at[src],
        g2s_v.at[pl.ds(0, NSRC - 1)],
        13,
    )
    g2s_v[src] = g2_v[eight((x % 2) * NSRC + src), :]

    for b in range(SRC_DEV // SRC_BLK):
        keep = blk_ref[0, b].astype(F32)
        rows = slice(b * SRC_BLK, (b + 1) * SRC_BLK)
        low_v[rows, :] = (raw_v[rows, :] * keep).astype(BF16)

    def mic_part(kk, acc):
        left = xt_v[pl.ds(kk * 8, 8)].reshape(8 * MIC_DEV, SRC_DEV)
        prod = jnp.dot(left, low_v[...], preferred_element_type=F32)
        for i in range(8):
            piece = prod[i * MIC_DEV : (i + 1) * MIC_DEV, :]
            p_v[kk * 8 + i] = piece
            acc = acc + time_ref[pl.ds(kk * 8 + i, 1), :] * piece
        return acc

    mm_v[...] = lax.fori_loop(0, SAMPLES // 8, mic_part, jnp.zeros((MIC_DEV, RANK), F32))

    def sixteen(k):
        return pl.ds(pl.multiple_of(k * 16, 16), 16)

    mic_rows = sixteen(src)
    send_src(
        lambda ss: mm_v.at[sixteen(ss), :], mr_v.at[src], mr_v.at[pl.ds(0, NSRC - 1)], 15
    )
    mr_v[src] = mm_v[mic_rows, :]
    yield waiting
    arrived(13)
    g2p_v[...] = jnp.sum(g2s_v[...], axis=0)
    send_xs(g2p_v, g2a_v, 14)
    arrived(15)
    m16_v[...] = jnp.sum(mr_v[...], axis=0)
    send_xs(m16_v, mall_v, 16)
    arrived(14)
    yield waiting
    gram_src = g2a_v[...].reshape(RANK, RANK)
    src_row, src_col = scales_of(gram_src, SRC_ALL)
    gram_src = gram_src / (src_row * src_col)
    gn_v[...] = gram_src
    a_v[...] = gram_src * gt_v[...] * (1.0 / (SRC_ALL * SAMPLES))
    invert(a_v)
    yield waiting
    arrived(16)
    mraw = -exact_dot(mall_v[...].reshape(NX * MIC_DEV, RANK) / src_row, a_v[...])
    mraw_v[...] = mraw

    g3_v[...] = exact_dot(mraw_v[:, core_lanes], mraw, ((0,), (0,)))
    g3s_v[...] = g3_v[eight(q), :]
    corner_z(g3s_v, c3_v, d3_v, c3z_v, d3z_v, 25)

    mic_own = pl.ds(pl.multiple_of(x * MIC_DEV, MIC_DEV), MIC_DEV)

    def time_part(k, c):
        t_v[k] = jnp.sum(p_v[k] * mraw_v[mic_own, :], axis=0, keepdims=True)
        return c

    lax.fori_loop(0, SAMPLES, time_part, 0)
    expect(20, ts_v.at[pl.ds(0, NXS - 1)])

    def send_sample(i, c):
        xx, ss = plane_step(i)
        send(t_v.at[xx * NSRC + ss], ts_v.at[p], 20, at(z, xx, ss))
        return c

    lax.fori_loop(0, NXS - 1, send_sample, 0)
    ts_v[p] = t_v[p]
    yield waiting

    raw_v[...] = raw_v[...] / src_row
    store_src = pltpu.make_async_copy(raw_v, src_out, load_sem.at[0])
    store_src.start()
    arrived(20)
    tp_v[...] = jnp.sum(ts_v[...], axis=0)
    send_z(tp_v, tz_v, 21)
    corner_sum(c3s_v, d3s_v, c3z_v, d3z_v, 25)
    yield waiting
    corner_xs(c3s_v, d3s_v, c3a_v, d3a_v, 18)
    arrived(21)
    tq_v[...] = jnp.sum(tz_v[...], axis=0)
    send_xs(tq_v, ta_v, 22)
    gram_mic = corner_gram(c3a_v, d3a_v, 18)
    yield waiting

    mic_row, mic_col = scales_of(gram_mic, MIC_ALL)
    a_v[...] = gn_v[...] * (gram_mic / (mic_row * mic_col)) * (1.0 / (SRC_ALL * MIC_ALL))
    mraw_v[mic_own, :] = mraw_v[mic_own, :] / mic_row
    store_mic = pltpu.make_async_copy(mraw_v.at[mic_own, :], mic_out, load_sem.at[1])
    store_mic.start()
    invert(a_v)
    yield waiting

    arrived(22)
    total = ta_v[...].reshape(SAMPLES, RANK)
    total = total / (src_row * mic_row)
    time_raw = -exact_dot(total, a_v[...])
    time_diag = jnp.sum(time_raw * time_raw, axis=0, keepdims=True)
    time_v[...] = time_raw / jnp.sqrt(time_diag / SAMPLES + 1e-06)
    store_time = pltpu.make_async_copy(time_v, time_out, load_sem.at[2])
    store_time.start()
    store_src.wait()
    store_mic.wait()
    store_time.wait()

    yield waiting


def kernel(*refs, stop=None):
    send_sem, recv_sem = refs[-2:]
    for count, waiting in enumerate(sweep(*refs)):
        if count == stop:
            break
    for stage, (receive, leave, coming) in waiting.items():
        if coming:
            receive(recv_sem.at[stage])
        leave(send_sem.at[stage])


def copy_out(src_in, mic_in, time_in, src_out, mic_out, time_out):
    src_out[...] = src_in[...]
    mic_out[...] = mic_in[...]
    time_out[...] = time_in[...]


def on_device(tensor_slab, observed_blocks, mic_factor, time_factor, stop=None, collective_id=0, name=None):
    hbm = pl.BlockSpec(memory_space=pltpu.HBM)
    outs = (
        jax.ShapeDtypeStruct((SRC_DEV, RANK), F32),
        jax.ShapeDtypeStruct((MIC_DEV, RANK), F32),
        jax.ShapeDtypeStruct((SAMPLES, RANK), F32),
    )
    results = pl.pallas_call(
        functools.partial(kernel, stop=stop),
        name=name,
        out_shape=outs,
        in_specs=[hbm] * 4,
        out_specs=(hbm,) * 3,
        scratch_shapes=[
            pltpu.SMEM((1, SRC_DEV // SRC_BLK), jnp.int32),
            pltpu.VMEM((MIC_DEV, RANK), F32),
            pltpu.VMEM((SAMPLES, RANK), F32),
            pltpu.VMEM((SAMPLES, SRC_DEV, MIC_DEV), BF16),
            pltpu.VMEM((SAMPLES, MIC_DEV, SRC_DEV), BF16),
            pltpu.VMEM((SAMPLES * MIC_DEV, RANK), BF16),
            pltpu.VMEM((SAMPLES, MIC_DEV, RANK), F32),
            pltpu.VMEM((SRC_DEV, RANK), F32),
            pltpu.VMEM((NX - 1, 128, RANK), F32),
            pltpu.VMEM((128, RANK), F32),
            pltpu.VMEM((NZ, 8, RANK), F32),
            pltpu.VMEM((SRC_DEV, RANK), F32),
            pltpu.VMEM((SRC_DEV, RANK), F32),
            pltpu.VMEM((SRC_DEV, RANK), BF16),
            pltpu.VMEM((RANK, RANK), F32),
            pltpu.VMEM((RANK, RANK), F32),
            pltpu.VMEM((RANK, RANK), F32),
            pltpu.VMEM((RANK, RANK), F32),
            pltpu.VMEM((NX, 8, RANK), F32),
            pltpu.VMEM((8, RANK), F32),
            pltpu.VMEM((8, 128), F32),
            pltpu.VMEM((8, 128), F32),
            pltpu.VMEM((NZ, 8, 128), F32),
            pltpu.VMEM((NZ, 8, 128), F32),
            pltpu.VMEM((8, 128), F32),
            pltpu.VMEM((8, 128), F32),
            pltpu.VMEM((NXS, 8, 128), F32),
            pltpu.VMEM((NXS // 2, 8, 128), F32),
            pltpu.VMEM((128, RANK), F32),
            pltpu.VMEM((NSRC, 8, RANK), F32),
            pltpu.VMEM((8, RANK), F32),
            pltpu.VMEM((NXS, 8, RANK), F32),
            pltpu.VMEM((MIC_DEV, RANK), F32),
            pltpu.VMEM((NSRC, 16, RANK), F32),
            pltpu.VMEM((16, RANK), F32),
            pltpu.VMEM((NXS, 16, RANK), F32),
            pltpu.VMEM((NX * MIC_DEV, RANK), F32),
            pltpu.VMEM((128, RANK), F32),
            pltpu.VMEM((8, RANK), F32),
            pltpu.VMEM((8, 128), F32),
            pltpu.VMEM((8, 128), F32),
            pltpu.VMEM((NZ, 8, 128), F32),
            pltpu.VMEM((NZ, 8, 128), F32),
            pltpu.VMEM((8, 128), F32),
            pltpu.VMEM((8, 128), F32),
            pltpu.VMEM((NXS, 8, 128), F32),
            pltpu.VMEM((NXS // 2, 8, 128), F32),
            pltpu.VMEM((NXS, 1, RANK), F32),
            pltpu.VMEM((NXS, 1, RANK), F32),
            pltpu.VMEM((1, RANK), F32),
            pltpu.VMEM((NZ, 1, RANK), F32),
            pltpu.VMEM((1, RANK), F32),
            pltpu.VMEM((NXS, 1, RANK), F32),
            pltpu.VMEM((SAMPLES, RANK), F32),
            pltpu.SemaphoreType.DMA((4,)),
            pltpu.SemaphoreType.DMA((STAGES,)),
            pltpu.SemaphoreType.DMA((STAGES,)),
        ],
        compiler_params=pltpu.CompilerParams(
            collective_id=collective_id, has_side_effects=True, vmem_limit_bytes=60 * 1024 * 1024
        ),
    )(tensor_slab, observed_blocks.reshape(1, SRC_DEV // SRC_BLK), mic_factor, time_factor)
    vmem = pl.BlockSpec(memory_space=pltpu.VMEM)
    return pl.pallas_call(
        copy_out,
        out_shape=outs,
        in_specs=[vmem] * 3,
        out_specs=(vmem,) * 3,
        compiler_params=pltpu.CompilerParams(vmem_limit_bytes=60 * 1024 * 1024),
    )(*results)


def solution(mesh):
    placed = (P(None, "src", "mic"), P("src", "mic"), P("mic", None), P())
    return jax.shard_map(
        on_device,
        mesh=mesh,
        in_specs=placed,
        out_specs=(P("src", None), P("mic", None), P()),
        check_vma=False,
    )
```

```python
import functools

import jax
import jax.numpy as jnp
from jax import lax
from jax.experimental import pallas as pl
from jax.experimental.pallas import tpu as pltpu
from jax.sharding import PartitionSpec as P

MESH = pl.DeviceIdType.MESH
F32 = jnp.float32
BF16 = jnp.bfloat16

RANK = 256
SAMPLES = 32
SRC_DEV = 512
MIC_DEV = 128
SRC_BLK = 64
NX = 4
NZ = 16
NSRC = 8
NXS = NX * NSRC
SRC_ALL = SRC_DEV * NSRC
MIC_ALL = MIC_DEV * NX * NZ
BLK = 32
STAGES = 27


def exact_dot(a, b, dims=((1,), (0,))):
    return lax.dot_general(
        a, b, (dims, ((), ())), precision=lax.Precision.HIGHEST, preferred_element_type=F32
    )


def split3(a):
    first = a.astype(BF16)
    rest = a - first.astype(F32)
    second = rest.astype(BF16)
    third = (rest - second.astype(F32)).astype(BF16)
    return first, second, third


def outer_dot(a, b):
    a0, a1, a2 = split3(a)
    b0, b1, b2 = split3(b)
    left = jnp.concatenate([a0, a0, a1, a1, a0, a2], axis=0)
    right = jnp.concatenate([b0, b1, b0, b1, b2, b0], axis=0)
    return lax.dot_general(left, right, (((0,), (0,)), ((), ())), preferred_element_type=F32)


def twice(v):
    return jnp.concatenate([v, v], axis=1)


def eliminate(panel, rel, tile, first, unit):
    sub = lax.broadcasted_iota(jnp.int32, (8, RANK), 0)
    sub_tile = lax.broadcasted_iota(jnp.int32, (8, 128), 0)
    groups = BLK // 8
    rows = [panel[8 * g : 8 * g + 8, :] for g in range(groups)]
    z_parts, w_parts = [], []
    for b in range(groups):
        lo = first + 8 * b
        col = {}
        for g in range(b, groups):
            part = rows[g][:, 128 * tile : 128 * tile + 128]
            col[g] = [jnp.broadcast_to(part[:, lo + j : lo + j + 1], (8, 128)) for j in range(8)]
        s = {}
        for k in range(8):
            for l in range(k, 8):
                s[k, l] = jnp.broadcast_to(col[b][l][k : k + 1, :], (8, 128))
        inside = (rel >= 8 * b) & (rel < 8 * b + 8)
        own = jnp.where(inside, jnp.where(rel == sub + 8 * b, unit, 0.0), rows[b])
        for g in range(b + 1, groups):
            rows[g] = jnp.where(inside, 0.0, rows[g])
        r = [jnp.broadcast_to(own[k : k + 1, :], (8, RANK)) for k in range(8)]
        inv = [None] * 8
        for j in range(0, 8, 2):
            a, m, d = s[j, j], s[j, j + 1], s[j + 1, j + 1]
            inv_det = 1.0 / (a * d - m * m)
            inv_a = 1.0 / a
            later = range(j + 2, 8)
            x = {l: s[j, l] for l in later}
            y = {l: s[j + 1, l] for l in later}
            u = {l: d * x[l] - m * y[l] for l in later}
            v = {l: a * y[l] - m * x[l] for l in later}
            for k in later:
                for l in range(k, 8):
                    s[k, l] = s[k, l] - (u[k] * x[l] + v[k] * y[l]) * inv_det
            f = m * inv_a
            r[j + 1] = r[j + 1] - twice(f) * r[j]
            inv[j] = inv_a
            inv[j + 1] = a * inv_det
            for k in later:
                r[k] = r[k] - twice(x[k] * inv_a) * r[j] - twice(v[k] * inv_det) * r[j + 1]
            for g in range(b + 1, groups):
                c1 = (col[g][j + 1] - col[g][j] * f) * inv[j + 1]
                c0 = col[g][j] * inv_a
                rows[g] = rows[g] - twice(c0) * r[j] - twice(c1) * r[j + 1]
                for l in later:
                    col[g][l] = col[g][l] - c0 * x[l] - c1 * (v[l] * inv_a)
        z, w = r[0], inv[0]
        for k in range(1, 8):
            z = jnp.where(sub == k, r[k], z)
            w = jnp.where(sub_tile == k, inv[k], w)
        z = jnp.where((rel >= 8 * b + 8) & (rel < BLK), 0.0, z)
        z_parts.append(z)
        w_parts.append(z * twice(w))
    return jnp.concatenate(z_parts, axis=0), jnp.concatenate(w_parts, axis=0)


def invert_block(a_ref, i):
    lane = lax.broadcasted_iota(jnp.int32, (8, RANK), 1)
    lane_row = lax.broadcasted_iota(jnp.int32, (1, RANK), 1)
    base = i * BLK
    rows = slice(base, base + BLK)
    z, w = eliminate(a_ref[rows, :], lane - base, base // 128, base % 128, -1.0)
    inside = (lane_row >= base) & (lane_row < base + BLK)
    update = outer_dot(z, w)
    a_ref[rows, :] = jnp.zeros((BLK, RANK), F32)
    a_ref[...] = jnp.where(inside, 0.0, a_ref[...]) - update


def invert(a_ref, between=None):
    for i in range(RANK // BLK):
        invert_block(a_ref, i)
        if between is not None and i in between:
            between[i]()


def factor(a_ref, z_ref, w_ref):
    lane = lax.broadcasted_iota(jnp.int32, (8, RANK), 1)
    lane_row = lax.broadcasted_iota(jnp.int32, (1, RANK), 1)
    for base in range(0, RANK, BLK):
        end = base + BLK
        rows = slice(base, end)
        z, w = eliminate(a_ref[rows, :], lane - base, base // 128, base % 128, 1.0)
        done = lane_row < end
        z_ref[rows, :] = jnp.where(done, z, 0.0)
        w_ref[rows, :] = jnp.where(done, w, 0.0)
        if end < RANK:
            left = end // 128 * 128
            inside = (lane_row >= base) & done
            update = outer_dot(z[:, left:], w)[end - left :, :]
            a_ref[end:, :] = jnp.where(inside, 0.0, a_ref[end:, :]) - update


def diagonal(gram):
    rows = lax.broadcasted_iota(jnp.int32, (RANK, RANK), 0)
    cols = lax.broadcasted_iota(jnp.int32, (RANK, RANK), 1)
    only = jnp.where(rows == cols, gram, 0.0)
    return jnp.sum(only, axis=0, keepdims=True), jnp.sum(only, axis=1, keepdims=True)


def scales_of(gram, count):
    row, col = diagonal(gram)
    return jnp.sqrt(row / count + 1e-06), jnp.sqrt(col / count + 1e-06)


def drain(ref, sem):
    pltpu.make_async_copy(ref, ref, sem).wait()


def ring_step(i, size=NZ):
    half = (i + 1) // 2
    return size // 2 + half - 2 * half * (i % 2)


def eight(k):
    return pl.ds(pl.multiple_of(k * 8, 8), 8)


def sweep(
    x_hbm,
    blk_hbm,
    mic_hbm,
    time_hbm,
    src_out,
    mic_out,
    time_out,
    blk_ref,
    mic_ref,
    time_ref,
    x_v,
    xt_v,
    kr_v,
    p_v,
    y_v,
    yx_v,
    y128_v,
    yz_v,
    yall_v,
    raw_v,
    low_v,
    gt_v,
    a_v,
    gn_v,
    zf_v,
    wf_v,
    g1_v,
    g1x_v,
    g1s_v,
    c1_v,
    d1_v,
    c1z_v,
    d1z_v,
    c1s_v,
    d1s_v,
    c1a_v,
    d1a_v,
    g2_v,
    g2s_v,
    g2p_v,
    g2a_v,
    mm_v,
    mr_v,
    m16_v,
    mall_v,
    mraw_v,
    g3_v,
    g3s_v,
    c3_v,
    d3_v,
    c3z_v,
    d3z_v,
    c3s_v,
    d3s_v,
    c3a_v,
    d3a_v,
    t_v,
    ts_v,
    tp_v,
    tz_v,
    tq_v,
    ta_v,
    time_v,
    relay_sem,
    load_sem,
    send_sem,
    recv_sem,
):
    me_mic = lax.axis_index("mic")
    src = lax.axis_index("src")
    z = me_mic // NX
    x = me_mic % NX
    p = x * NSRC + src
    core = src % 2
    q = p // 2

    def at(zz, xx, ss):
        return (zz * NX + xx, ss)

    load_mic = pltpu.make_async_copy(mic_hbm, mic_ref, load_sem.at[0])
    load_time = pltpu.make_async_copy(time_hbm, time_ref, load_sem.at[1])
    load_blk = pltpu.make_async_copy(blk_hbm, blk_ref, load_sem.at[2])
    load = pltpu.make_async_copy(x_hbm, x_v, load_sem.at[3])
    load_mic.start()
    load_time.start()
    load_blk.start()
    load.start()

    barrier = pltpu.get_barrier_semaphore()

    def greet_z(i, c):
        zz = (z + ring_step(i)) % NZ
        pl.semaphore_signal(barrier, inc=1, device_id=at(zz, x, src), device_id_type=MESH)
        return c

    def greet_xs(d, c):
        q = (p + d) % NXS
        pl.semaphore_signal(
            barrier, inc=1, device_id=at(z, q // NSRC, q % NSRC), device_id_type=MESH
        )
        return c

    lax.fori_loop(NZ // 2 - 1, NZ - 1, greet_z, 0)
    lax.fori_loop(1, NXS, greet_xs, 0)

    waiting = {}

    def expect(stage, ref):
        waiting[stage] = [lambda sem: drain(ref, sem), lambda sem: drain(ref, sem), True]

    def expect_by_core(stage, received, sent):
        def by_core(refs):
            def wait(sem):
                for which in range(2):
                    if refs[which] is not None:
                        pl.when(core == which)(functools.partial(drain, refs[which], sem))

            return wait

        waiting[stage] = [by_core(received), by_core(sent), True]

    def arrived(stage):
        waiting[stage][0](recv_sem.at[stage])
        waiting[stage][2] = False

    def send(src_ref, dst_ref, stage, device):
        pltpu.make_async_remote_copy(
            src_ref=src_ref,
            dst_ref=dst_ref,
            send_sem=send_sem.at[stage],
            recv_sem=recv_sem.at[stage],
            device_id=device,
            device_id_type=MESH,
        ).start()

    def send_x(gram_ref, dst, stage):
        expect(stage, dst.at[pl.ds(0, NX - 1)])

        def one(i, c):
            xx = (x + ring_step(i, NX)) % NX
            rows = eight(core * 16 + (xx * NSRC + src) // 2)
            send(gram_ref.at[rows, :], dst.at[x], stage, at(z, xx, src))
            return c

        lax.fori_loop(0, NX - 1, one, 0)
        dst[x] = gram_ref[eight(core * 16 + q), :]

    def send_z(piece_ref, dst, stage):
        expect(stage, dst.at[pl.ds(0, NZ - 1)])

        def one(i, c):
            send(piece_ref, dst.at[z], stage, at((z + ring_step(i)) % NZ, x, src))
            return c

        lax.fori_loop(0, NZ - 1, one, 0)
        dst[z] = piece_ref[...]

    def plane_step(i):
        xx = (x + ring_step(i // NSRC, NX)) % NX
        yy = (src // 2 + ring_step(i // 2 % (NSRC // 2), NSRC // 2)) % (NSRC // 2)
        return xx, yy * 2 + (src % 2 + 1 + i) % 2

    def send_xs(piece_ref, dst, stage):
        expect(stage, dst.at[pl.ds(0, NXS - 1)])

        def one(i, c):
            xx, ss = plane_step(i)
            send(piece_ref, dst.at[p], stage, at(z, xx, ss))
            return c

        lax.fori_loop(0, NXS - 1, one, 0)
        dst[p] = piece_ref[...]

    core_lanes = pl.ds(pl.multiple_of(core * 128, 128), 128)

    def corner_z(piece_ref, one_v, two_v, one_z, two_z, stage):
        one_v[...] = piece_ref[:, core_lanes]
        send_z(one_v, one_z, stage)
        half = two_z.at[pl.ds(0, NZ - 1)]

        @pl.when(core == 0)
        def _():
            two_v[...] = piece_ref[:, 128:]
            send_z(two_v, two_z, stage + 1)

        expect_by_core(stage + 1, (half, None), (half, None))

    def corner_sum(one_v, two_v, one_z, two_z, stage):
        arrived(stage)
        one_v[...] = jnp.sum(one_z[...], axis=0)
        arrived(stage + 1)

        @pl.when(core == 0)
        def _():
            two_v[...] = jnp.sum(two_z[...], axis=0)

    def corner_xs(one_v, two_v, one_a, two_a, stage):
        send_xs(one_v, one_a, stage)

        @pl.when(core == 0)
        def _():
            def one(i, c):
                xx, ss = plane_step(i)
                send(two_v, two_a.at[q], stage + 1, at(z, xx, ss))
                return c

            lax.fori_loop(0, NXS - 1, one, 0)
            two_a[q] = two_v[...]

        expect_by_core(
            stage + 1,
            (two_a.at[pl.ds(0, NXS // 2 - 1)], two_a),
            (one_a.at[pl.ds(0, NXS - 1)], None),
        )

    def corner_gram(one_a, two_a, stage):
        arrived(stage)
        arrived(stage + 1)
        ones = one_a[...].reshape(NXS // 2, 2, 8, 128)
        upper = two_a[...].reshape(128, 128)
        return jnp.concatenate(
            [
                jnp.concatenate([ones[:, 0].reshape(128, 128), upper], axis=1),
                jnp.concatenate([upper.T, ones[:, 1].reshape(128, 128)], axis=1),
            ],
            axis=0,
        )

    def send_src(piece_of, dst_ref, expected, stage):
        expect(stage, expected)

        def one(i, c):
            ss = plane_step(NXS - NSRC + i)[1]
            send(piece_of(ss), dst_ref, stage, at(z, x, ss))
            return c

        lax.fori_loop(0, NSRC - 1, one, 0)

    load_mic.wait()
    load_time.wait()
    mic = mic_ref[...]
    g1_v[...] = exact_dot(mic, mic, ((0,), (0,)))
    times = time_ref[...]
    gt_v[...] = exact_dot(times, times, ((0,), (0,)))
    mic_low = mic.astype(BF16).astype(F32)

    def make_kr(k, c):
        kr_v[pl.ds(pl.multiple_of(k * MIC_DEV, MIC_DEV), MIC_DEV), :] = (
            time_ref[pl.ds(k, 1), :] * mic_low
        ).astype(BF16)
        return c

    lax.fori_loop(0, SAMPLES, make_kr, 0)

    load_blk.wait()
    load.wait()
    for xx in range(NX):
        left = jnp.concatenate(
            [x_v[k, xx * 128 : (xx + 1) * 128, :] for k in range(SAMPLES)], axis=1
        )
        part = jnp.dot(left, kr_v[...], preferred_element_type=F32)
        for h in range(2):
            keep = blk_ref[0, xx * 2 + h].astype(F32)
            rows = slice(xx * 128 + h * 64, xx * 128 + (h + 1) * 64)
            y_v[rows, :] = part[h * 64 : (h + 1) * 64, :] * keep

    pl.semaphore_wait(barrier, NZ // 2 + NXS - 1)

    for step in (NZ // 4, NZ - NZ // 4):
        pl.semaphore_signal(
            relay_sem, inc=1, device_id=at((z + step) % NZ, x, src), device_id_type=MESH
        )
    yield waiting

    send_x(g1_v, g1x_v, 0)

    for g in range(4):
        expect(3 + g, yx_v.at[0, pl.ds(0, 96), :])

        def row_group(ix, c, g=g):
            dx = ring_step(ix, NX)
            xx = (x + dx) % NX

            def one(i, c):
                zz = (z + ring_step(i)) % NZ
                send(
                    y_v.at[eight(xx * NZ + zz), :],
                    yx_v.at[dx - 1, eight(zz), :],
                    3 + g,
                    at(z, xx, src),
                )
                return c

            return lax.fori_loop(4 * g, 4 * g + 4, one, c)

        lax.fori_loop(0, NX - 1, row_group, 0)

    arrived(0)
    g1s_v[...] = (g1x_v[0] + g1x_v[1]) + (g1x_v[2] + g1x_v[3])
    pl.semaphore_wait(relay_sem, 2)
    corner_z(g1s_v, c1_v, d1_v, c1z_v, d1z_v, 23)

    expect(7, yz_v.at[pl.ds(0, NZ - 1)])
    for g in range(4):
        arrived(3 + g)

        def sum_send(i, c):
            zz = (z + ring_step(i)) % NZ
            rows = eight(zz)
            y128_v[rows, :] = (y_v[eight(x * NZ + zz), :] + yx_v[0, rows, :]) + (
                yx_v[1, rows, :] + yx_v[2, rows, :]
            )
            send(y128_v.at[rows, :], yz_v.at[i], 7, at(zz, x, src))
            return c

        lax.fori_loop(4 * g, min(4 * g + 4, NZ - 1), sum_send, 0)
    own = eight(z)
    yz_v[NZ - 1] = (y_v[eight(x * NZ + z), :] + yx_v[0, own, :]) + (
        yx_v[1, own, :] + yx_v[2, own, :]
    )
    yield waiting


    corner_sum(c1s_v, d1s_v, c1z_v, d1z_v, 23)
    corner_xs(c1s_v, d1s_v, c1a_v, d1a_v, 1)

    arrived(7)
    mine = eight(x * NZ + z)
    yall_v[mine, :] = jnp.sum(yz_v[...], axis=0)
    for g in range(4):
        last = min(4 * g + 4, NZ - 1)
        expect(8 + g, yall_v.at[pl.ds(0, 8 * (last - 4 * g)), :])

        def back_z(i, c, g=g):
            zz = (z + ring_step(i)) % NZ
            send(yall_v.at[mine, :], yall_v.at[mine, :], 8 + g, at(zz, x, src))
            return c

        lax.fori_loop(4 * g, last, back_z, 0)

    expect(12, yall_v.at[pl.ds(0, 128 * (NX - 1)), :])

    def forward(rows):
        def one(ix, c):
            xx = (x + ring_step(ix, NX)) % NX
            send(yall_v.at[rows, :], yall_v.at[rows, :], 12, at(z, xx, src))
            return c

        lax.fori_loop(0, NX - 1, one, 0)

    def forward_group(g):
        arrived(8 + g)

        def one(i, c):
            forward(eight(x * NZ + (z + NZ - ring_step(i)) % NZ))
            return c

        lax.fori_loop(4 * g, min(4 * g + 4, NZ - 1), one, 0)

    forward(mine)
    yield waiting

    def flip(k, c):
        xt_v[k] = x_v[k].T
        return c

    lax.fori_loop(0, SAMPLES, flip, 0)

    forward_group(3)
    forward_group(2)
    gram_mic = corner_gram(c1a_v, d1a_v, 1)
    yield waiting
    a_v[...] = gram_mic * gt_v[...] * (1.0 / (MIC_ALL * SAMPLES))
    invert(a_v, {1: lambda: forward_group(1), 3: lambda: forward_group(0)})
    yield waiting
    arrived(12)
    yield waiting
    raw = -exact_dot(yall_v[...], a_v[...])
    raw_v[...] = raw

    half = x // 2
    half_lanes = pl.ds(pl.multiple_of(half * 128, 128), 128)
    g2_v[...] = exact_dot(raw_v[:, half_lanes], raw, ((0,), (0,)))
    send_src(
        lambda ss: g2_v.at[eight((x % 2) * NSRC + ss), :],
        g2s_v.at[src],
        g2s_v.at[pl.ds(0, NSRC - 1)],
        13,
    )
    g2s_v[src] = g2_v[eight((x % 2) * NSRC + src), :]

    for b in range(SRC_DEV // SRC_BLK):
        keep = blk_ref[0, b].astype(F32)
        rows = slice(b * SRC_BLK, (b + 1) * SRC_BLK)
        low_v[rows, :] = (raw_v[rows, :] * keep).astype(BF16)

    def mic_part(kk, acc):
        left = xt_v[pl.ds(kk * 8, 8)].reshape(8 * MIC_DEV, SRC_DEV)
        prod = jnp.dot(left, low_v[...], preferred_element_type=F32)
        for i in range(8):
            piece = prod[i * MIC_DEV : (i + 1) * MIC_DEV, :]
            p_v[kk * 8 + i] = piece
            acc = acc + time_ref[pl.ds(kk * 8 + i, 1), :] * piece
        return acc

    mm_v[...] = lax.fori_loop(0, SAMPLES // 8, mic_part, jnp.zeros((MIC_DEV, RANK), F32))

    def sixteen(k):
        return pl.ds(pl.multiple_of(k * 16, 16), 16)

    mic_rows = sixteen(src)
    send_src(
        lambda ss: mm_v.at[sixteen(ss), :], mr_v.at[src], mr_v.at[pl.ds(0, NSRC - 1)], 15
    )
    mr_v[src] = mm_v[mic_rows, :]
    yield waiting
    arrived(13)
    g2p_v[...] = jnp.sum(g2s_v[...], axis=0)
    send_xs(g2p_v, g2a_v, 14)
    arrived(15)
    m16_v[...] = jnp.sum(mr_v[...], axis=0)
    send_xs(m16_v, mall_v, 16)
    arrived(14)
    yield waiting
    gram_src = g2a_v[...].reshape(RANK, RANK)
    src_row, src_col = scales_of(gram_src, SRC_ALL)
    gram_src = gram_src / (src_row * src_col)
    gn_v[...] = gram_src
    a_v[...] = gram_src * gt_v[...] * (1.0 / (SRC_ALL * SAMPLES))
    invert(a_v)
    yield waiting
    arrived(16)
    mraw = -exact_dot(mall_v[...].reshape(NX * MIC_DEV, RANK) / src_row, a_v[...])
    mraw_v[...] = mraw

    g3_v[...] = exact_dot(mraw_v[:, core_lanes], mraw, ((0,), (0,)))
    g3s_v[...] = g3_v[eight(q), :]
    corner_z(g3s_v, c3_v, d3_v, c3z_v, d3z_v, 25)

    mic_own = pl.ds(pl.multiple_of(x * MIC_DEV, MIC_DEV), MIC_DEV)

    def time_part(k, c):
        t_v[k] = jnp.sum(p_v[k] * mraw_v[mic_own, :], axis=0, keepdims=True)
        return c

    lax.fori_loop(0, SAMPLES, time_part, 0)
    expect(20, ts_v.at[pl.ds(0, NXS - 1)])

    def send_sample(i, c):
        xx, ss = plane_step(i)
        send(t_v.at[xx * NSRC + ss], ts_v.at[p], 20, at(z, xx, ss))
        return c

    lax.fori_loop(0, NXS - 1, send_sample, 0)
    ts_v[p] = t_v[p]
    yield waiting

    raw_v[...] = raw_v[...] / src_row
    store_src = pltpu.make_async_copy(raw_v, src_out, load_sem.at[0])
    store_src.start()
    arrived(20)
    tp_v[...] = jnp.sum(ts_v[...], axis=0)
    send_z(tp_v, tz_v, 21)
    corner_sum(c3s_v, d3s_v, c3z_v, d3z_v, 25)
    yield waiting
    corner_xs(c3s_v, d3s_v, c3a_v, d3a_v, 18)
    arrived(21)
    tq_v[...] = jnp.sum(tz_v[...], axis=0)
    send_xs(tq_v, ta_v, 22)
    gram_mic = corner_gram(c3a_v, d3a_v, 18)
    yield waiting

    mic_row, mic_col = scales_of(gram_mic, MIC_ALL)
    a_v[...] = gn_v[...] * (gram_mic / (mic_row * mic_col)) * (1.0 / (SRC_ALL * MIC_ALL))
    mraw_v[mic_own, :] = mraw_v[mic_own, :] / mic_row
    store_mic = pltpu.make_async_copy(mraw_v.at[mic_own, :], mic_out, load_sem.at[1])
    store_mic.start()
    factor(a_v, zf_v, wf_v)
    yield waiting

    arrived(22)
    total = ta_v[...].reshape(SAMPLES, RANK)
    total = total / (src_row * mic_row)
    time_raw = exact_dot(exact_dot(total, zf_v[...], ((1,), (1,))), wf_v[...])
    time_diag = jnp.sum(time_raw * time_raw, axis=0, keepdims=True)
    time_v[...] = time_raw / jnp.sqrt(time_diag / SAMPLES + 1e-06)
    store_time = pltpu.make_async_copy(time_v, time_out, load_sem.at[2])
    store_time.start()
    store_src.wait()
    store_mic.wait()
    store_time.wait()

    yield waiting


def kernel(*refs, stop=None):
    send_sem, recv_sem = refs[-2:]
    for count, waiting in enumerate(sweep(*refs)):
        if count == stop:
            break
    for stage, (receive, leave, coming) in waiting.items():
        if coming:
            receive(recv_sem.at[stage])
        leave(send_sem.at[stage])


def copy_out(src_in, mic_in, time_in, src_out, mic_out, time_out):
    src_out[...] = src_in[...]
    mic_out[...] = mic_in[...]
    time_out[...] = time_in[...]


def on_device(tensor_slab, observed_blocks, mic_factor, time_factor, stop=None, collective_id=0, name=None):
    hbm = pl.BlockSpec(memory_space=pltpu.HBM)
    outs = (
        jax.ShapeDtypeStruct((SRC_DEV, RANK), F32),
        jax.ShapeDtypeStruct((MIC_DEV, RANK), F32),
        jax.ShapeDtypeStruct((SAMPLES, RANK), F32),
    )
    results = pl.pallas_call(
        functools.partial(kernel, stop=stop),
        name=name,
        out_shape=outs,
        in_specs=[hbm] * 4,
        out_specs=(hbm,) * 3,
        scratch_shapes=[
            pltpu.SMEM((1, SRC_DEV // SRC_BLK), jnp.int32),
            pltpu.VMEM((MIC_DEV, RANK), F32),
            pltpu.VMEM((SAMPLES, RANK), F32),
            pltpu.VMEM((SAMPLES, SRC_DEV, MIC_DEV), BF16),
            pltpu.VMEM((SAMPLES, MIC_DEV, SRC_DEV), BF16),
            pltpu.VMEM((SAMPLES * MIC_DEV, RANK), BF16),
            pltpu.VMEM((SAMPLES, MIC_DEV, RANK), F32),
            pltpu.VMEM((SRC_DEV, RANK), F32),
            pltpu.VMEM((NX - 1, 128, RANK), F32),
            pltpu.VMEM((128, RANK), F32),
            pltpu.VMEM((NZ, 8, RANK), F32),
            pltpu.VMEM((SRC_DEV, RANK), F32),
            pltpu.VMEM((SRC_DEV, RANK), F32),
            pltpu.VMEM((SRC_DEV, RANK), BF16),
            pltpu.VMEM((RANK, RANK), F32),
            pltpu.VMEM((RANK, RANK), F32),
            pltpu.VMEM((RANK, RANK), F32),
            pltpu.VMEM((RANK, RANK), F32),
            pltpu.VMEM((RANK, RANK), F32),
            pltpu.VMEM((RANK, RANK), F32),
            pltpu.VMEM((NX, 8, RANK), F32),
            pltpu.VMEM((8, RANK), F32),
            pltpu.VMEM((8, 128), F32),
            pltpu.VMEM((8, 128), F32),
            pltpu.VMEM((NZ, 8, 128), F32),
            pltpu.VMEM((NZ, 8, 128), F32),
            pltpu.VMEM((8, 128), F32),
            pltpu.VMEM((8, 128), F32),
            pltpu.VMEM((NXS, 8, 128), F32),
            pltpu.VMEM((NXS // 2, 8, 128), F32),
            pltpu.VMEM((128, RANK), F32),
            pltpu.VMEM((NSRC, 8, RANK), F32),
            pltpu.VMEM((8, RANK), F32),
            pltpu.VMEM((NXS, 8, RANK), F32),
            pltpu.VMEM((MIC_DEV, RANK), F32),
            pltpu.VMEM((NSRC, 16, RANK), F32),
            pltpu.VMEM((16, RANK), F32),
            pltpu.VMEM((NXS, 16, RANK), F32),
            pltpu.VMEM((NX * MIC_DEV, RANK), F32),
            pltpu.VMEM((128, RANK), F32),
            pltpu.VMEM((8, RANK), F32),
            pltpu.VMEM((8, 128), F32),
            pltpu.VMEM((8, 128), F32),
            pltpu.VMEM((NZ, 8, 128), F32),
            pltpu.VMEM((NZ, 8, 128), F32),
            pltpu.VMEM((8, 128), F32),
            pltpu.VMEM((8, 128), F32),
            pltpu.VMEM((NXS, 8, 128), F32),
            pltpu.VMEM((NXS // 2, 8, 128), F32),
            pltpu.VMEM((NXS, 1, RANK), F32),
            pltpu.VMEM((NXS, 1, RANK), F32),
            pltpu.VMEM((1, RANK), F32),
            pltpu.VMEM((NZ, 1, RANK), F32),
            pltpu.VMEM((1, RANK), F32),
            pltpu.VMEM((NXS, 1, RANK), F32),
            pltpu.VMEM((SAMPLES, RANK), F32),
            pltpu.SemaphoreType.REGULAR,
            pltpu.SemaphoreType.DMA((4,)),
            pltpu.SemaphoreType.DMA((STAGES,)),
            pltpu.SemaphoreType.DMA((STAGES,)),
        ],
        compiler_params=pltpu.CompilerParams(
            collective_id=collective_id, has_side_effects=True, vmem_limit_bytes=60 * 1024 * 1024
        ),
    )(tensor_slab, observed_blocks.reshape(1, SRC_DEV // SRC_BLK), mic_factor, time_factor)
    vmem = pl.BlockSpec(memory_space=pltpu.VMEM)
    return pl.pallas_call(
        copy_out,
        out_shape=outs,
        in_specs=[vmem] * 3,
        out_specs=(vmem,) * 3,
        compiler_params=pltpu.CompilerParams(vmem_limit_bytes=60 * 1024 * 1024),
    )(*results)


def solution(mesh):
    placed = (P(None, "src", "mic"), P("src", "mic"), P("mic", None), P())
    return jax.shard_map(
        on_device,
        mesh=mesh,
        in_specs=placed,
        out_specs=(P("src", None), P("mic", None), P()),
        check_vma=False,
    )
```

```python
import functools

import jax
import jax.numpy as jnp
from jax import lax
from jax.experimental import pallas as pl
from jax.experimental.pallas import tpu as pltpu
from jax.sharding import PartitionSpec as P

MESH = pl.DeviceIdType.MESH
F32 = jnp.float32
BF16 = jnp.bfloat16

RANK = 256
SAMPLES = 32
SRC_DEV = 512
MIC_DEV = 128
SRC_BLK = 64
NX = 4
NZ = 16
NSRC = 8
NXS = NX * NSRC
SRC_ALL = SRC_DEV * NSRC
MIC_ALL = MIC_DEV * NX * NZ
BLK = 32
STAGES = 27


def exact_dot(a, b, dims=((1,), (0,))):
    return lax.dot_general(
        a, b, (dims, ((), ())), precision=lax.Precision.HIGHEST, preferred_element_type=F32
    )


def split3(a):
    first = a.astype(BF16)
    rest = a - first.astype(F32)
    second = rest.astype(BF16)
    third = (rest - second.astype(F32)).astype(BF16)
    return first, second, third


def outer_dot(a, b):
    a0, a1, a2 = split3(a)
    b0, b1, b2 = split3(b)
    left = jnp.concatenate([a0, a0, a1, a1, a0, a2], axis=0)
    right = jnp.concatenate([b0, b1, b0, b1, b2, b0], axis=0)
    return lax.dot_general(left, right, (((0,), (0,)), ((), ())), preferred_element_type=F32)


def twice(v):
    return jnp.concatenate([v, v], axis=1)


def eliminate(panel, rel, tile, first, unit):
    sub = lax.broadcasted_iota(jnp.int32, (8, RANK), 0)
    sub_tile = lax.broadcasted_iota(jnp.int32, (8, 128), 0)
    groups = BLK // 8
    rows = [panel[8 * g : 8 * g + 8, :] for g in range(groups)]
    z_parts, w_parts = [], []
    for b in range(groups):
        lo = first + 8 * b
        col = {}
        for g in range(b, groups):
            part = rows[g][:, 128 * tile : 128 * tile + 128]
            col[g] = [jnp.broadcast_to(part[:, lo + j : lo + j + 1], (8, 128)) for j in range(8)]
        s = {}
        for k in range(8):
            for l in range(k, 8):
                s[k, l] = jnp.broadcast_to(col[b][l][k : k + 1, :], (8, 128))
        inside = (rel >= 8 * b) & (rel < 8 * b + 8)
        own = jnp.where(inside, jnp.where(rel == sub + 8 * b, unit, 0.0), rows[b])
        for g in range(b + 1, groups):
            rows[g] = jnp.where(inside, 0.0, rows[g])
        r = [jnp.broadcast_to(own[k : k + 1, :], (8, RANK)) for k in range(8)]
        inv = [None] * 8
        for j in range(0, 8, 2):
            a, m, d = s[j, j], s[j, j + 1], s[j + 1, j + 1]
            inv_det = 1.0 / (a * d - m * m)
            inv_a = 1.0 / a
            later = range(j + 2, 8)
            x = {l: s[j, l] for l in later}
            y = {l: s[j + 1, l] for l in later}
            u = {l: d * x[l] - m * y[l] for l in later}
            v = {l: a * y[l] - m * x[l] for l in later}
            for k in later:
                for l in range(k, 8):
                    s[k, l] = s[k, l] - (u[k] * x[l] + v[k] * y[l]) * inv_det
            f = m * inv_a
            r[j + 1] = r[j + 1] - twice(f) * r[j]
            inv[j] = inv_a
            inv[j + 1] = a * inv_det
            for k in later:
                r[k] = r[k] - twice(x[k] * inv_a) * r[j] - twice(v[k] * inv_det) * r[j + 1]
            for g in range(b + 1, groups):
                c1 = (col[g][j + 1] - col[g][j] * f) * inv[j + 1]
                c0 = col[g][j] * inv_a
                rows[g] = rows[g] - twice(c0) * r[j] - twice(c1) * r[j + 1]
                for l in later:
                    col[g][l] = col[g][l] - c0 * x[l] - c1 * (v[l] * inv_a)
        z, w = r[0], inv[0]
        for k in range(1, 8):
            z = jnp.where(sub == k, r[k], z)
            w = jnp.where(sub_tile == k, inv[k], w)
        z = jnp.where((rel >= 8 * b + 8) & (rel < BLK), 0.0, z)
        z_parts.append(z)
        w_parts.append(z * twice(w))
    return jnp.concatenate(z_parts, axis=0), jnp.concatenate(w_parts, axis=0)


def invert_block(a_ref, i):
    lane = lax.broadcasted_iota(jnp.int32, (8, RANK), 1)
    lane_row = lax.broadcasted_iota(jnp.int32, (1, RANK), 1)
    base = i * BLK
    rows = slice(base, base + BLK)
    z, w = eliminate(a_ref[rows, :], lane - base, base // 128, base % 128, -1.0)
    inside = (lane_row >= base) & (lane_row < base + BLK)
    update = outer_dot(z, w)
    a_ref[rows, :] = jnp.zeros((BLK, RANK), F32)
    a_ref[...] = jnp.where(inside, 0.0, a_ref[...]) - update


def invert(a_ref, between=None):
    for i in range(RANK // BLK):
        invert_block(a_ref, i)
        if between is not None and i in between:
            between[i]()


def factor(a_ref, z_ref, w_ref, after_first):
    lane = lax.broadcasted_iota(jnp.int32, (8, RANK), 1)
    lane_row = lax.broadcasted_iota(jnp.int32, (1, RANK), 1)
    for base in range(0, RANK, BLK):
        end = base + BLK
        rows = slice(base, end)
        z, w = eliminate(a_ref[rows, :], lane - base, base // 128, base % 128, 1.0)
        done = lane_row < end
        z_ref[rows, :] = jnp.where(done, z, 0.0)
        w_ref[rows, :] = jnp.where(done, w, 0.0)
        if end < RANK:
            left = end // 128 * 128
            inside = (lane_row >= base) & done
            update = outer_dot(z[:, left:], w)[end - left :, :]
            a_ref[end:, :] = jnp.where(inside, 0.0, a_ref[end:, :]) - update
        if base == 0:
            after_first()


def diagonal(gram):
    rows = lax.broadcasted_iota(jnp.int32, (RANK, RANK), 0)
    cols = lax.broadcasted_iota(jnp.int32, (RANK, RANK), 1)
    only = jnp.where(rows == cols, gram, 0.0)
    return jnp.sum(only, axis=0, keepdims=True), jnp.sum(only, axis=1, keepdims=True)


def scales_of(gram, count):
    row, col = diagonal(gram)
    return jnp.sqrt(row / count + 1e-06), jnp.sqrt(col / count + 1e-06)


def drain(ref, sem):
    pltpu.make_async_copy(ref, ref, sem).wait()


def ring_step(i, size=NZ):
    half = (i + 1) // 2
    return size // 2 + half - 2 * half * (i % 2)


def eight(k):
    return pl.ds(pl.multiple_of(k * 8, 8), 8)


def sweep(
    x_hbm,
    blk_hbm,
    mic_hbm,
    time_hbm,
    src_out,
    mic_out,
    time_out,
    blk_ref,
    mic_ref,
    time_ref,
    x_v,
    xt_v,
    kr_v,
    p_v,
    y_v,
    yx_v,
    y128_v,
    yz_v,
    yall_v,
    raw_v,
    low_v,
    gt_v,
    a_v,
    gn_v,
    zf_v,
    wf_v,
    g1_v,
    g1x_v,
    g1s_v,
    c1_v,
    d1_v,
    c1z_v,
    d1z_v,
    c1s_v,
    d1s_v,
    c1a_v,
    d1a_v,
    g2_v,
    g2s_v,
    g2p_v,
    g2a_v,
    mm_v,
    mr_v,
    m16_v,
    mall_v,
    mraw_v,
    g3_v,
    g3s_v,
    c3_v,
    d3_v,
    c3z_v,
    d3z_v,
    c3s_v,
    d3s_v,
    c3a_v,
    d3a_v,
    t_v,
    ts_v,
    tp_v,
    tz_v,
    tq_v,
    ta_v,
    time_v,
    load_sem,
    send_sem,
    recv_sem,
):
    me_mic = lax.axis_index("mic")
    src = lax.axis_index("src")
    z = me_mic // NX
    x = me_mic % NX
    p = x * NSRC + src
    core = src % 2
    q = p // 2

    def at(zz, xx, ss):
        return (zz * NX + xx, ss)

    load_mic = pltpu.make_async_copy(mic_hbm, mic_ref, load_sem.at[0])
    load_time = pltpu.make_async_copy(time_hbm, time_ref, load_sem.at[1])
    load_blk = pltpu.make_async_copy(blk_hbm, blk_ref, load_sem.at[2])
    load = pltpu.make_async_copy(x_hbm, x_v, load_sem.at[3])
    load_mic.start()
    load_time.start()
    load_blk.start()
    load.start()

    barrier = pltpu.get_barrier_semaphore()

    def greet_z(i, c):
        zz = (z + ring_step(i)) % NZ
        pl.semaphore_signal(barrier, inc=1, device_id=at(zz, x, src), device_id_type=MESH)
        return c

    def greet_xs(d, c):
        q = (p + d) % NXS
        pl.semaphore_signal(
            barrier, inc=1, device_id=at(z, q // NSRC, q % NSRC), device_id_type=MESH
        )
        return c

    lax.fori_loop(0, NZ - 1, greet_z, 0)
    lax.fori_loop(1, NXS, greet_xs, 0)

    waiting = {}

    def expect(stage, ref):
        waiting[stage] = [lambda sem: drain(ref, sem), lambda sem: drain(ref, sem), True]

    def expect_by_core(stage, received, sent):
        def by_core(refs):
            def wait(sem):
                for which in range(2):
                    if refs[which] is not None:
                        pl.when(core == which)(functools.partial(drain, refs[which], sem))

            return wait

        waiting[stage] = [by_core(received), by_core(sent), True]

    def arrived(stage):
        waiting[stage][0](recv_sem.at[stage])
        waiting[stage][2] = False

    def send(src_ref, dst_ref, stage, device):
        pltpu.make_async_remote_copy(
            src_ref=src_ref,
            dst_ref=dst_ref,
            send_sem=send_sem.at[stage],
            recv_sem=recv_sem.at[stage],
            device_id=device,
            device_id_type=MESH,
        ).start()

    def send_x(gram_ref, dst, stage):
        expect(stage, dst.at[pl.ds(0, NX - 1)])

        def one(i, c):
            xx = (x + ring_step(i, NX)) % NX
            rows = eight(core * 16 + (xx * NSRC + src) // 2)
            send(gram_ref.at[rows, :], dst.at[x], stage, at(z, xx, src))
            return c

        lax.fori_loop(0, NX - 1, one, 0)
        dst[x] = gram_ref[eight(core * 16 + q), :]

    def send_z(piece_ref, dst, stage):
        expect(stage, dst.at[pl.ds(0, NZ - 1)])

        def one(i, c):
            send(piece_ref, dst.at[z], stage, at((z + ring_step(i)) % NZ, x, src))
            return c

        lax.fori_loop(0, NZ - 1, one, 0)
        dst[z] = piece_ref[...]

    def plane_step(i):
        xx = (x + ring_step(i // NSRC, NX)) % NX
        yy = (src // 2 + ring_step(i // 2 % (NSRC // 2), NSRC // 2)) % (NSRC // 2)
        return xx, yy * 2 + (src % 2 + 1 + i) % 2

    def send_xs(piece_ref, dst, stage):
        expect(stage, dst.at[pl.ds(0, NXS - 1)])

        def one(i, c):
            xx, ss = plane_step(i)
            send(piece_ref, dst.at[p], stage, at(z, xx, ss))
            return c

        lax.fori_loop(0, NXS - 1, one, 0)
        dst[p] = piece_ref[...]

    core_lanes = pl.ds(pl.multiple_of(core * 128, 128), 128)

    def corner_z(piece_ref, one_v, two_v, one_z, two_z, stage):
        one_v[...] = piece_ref[:, core_lanes]
        send_z(one_v, one_z, stage)
        half = two_z.at[pl.ds(0, NZ - 1)]

        @pl.when(core == 0)
        def _():
            two_v[...] = piece_ref[:, 128:]
            send_z(two_v, two_z, stage + 1)

        expect_by_core(stage + 1, (half, None), (half, None))

    def corner_sum(one_v, two_v, one_z, two_z, stage):
        arrived(stage)
        one_v[...] = jnp.sum(one_z[...], axis=0)
        arrived(stage + 1)

        @pl.when(core == 0)
        def _():
            two_v[...] = jnp.sum(two_z[...], axis=0)

    def corner_xs(one_v, two_v, one_a, two_a, stage):
        send_xs(one_v, one_a, stage)

        @pl.when(core == 0)
        def _():
            def one(i, c):
                xx, ss = plane_step(i)
                send(two_v, two_a.at[q], stage + 1, at(z, xx, ss))
                return c

            lax.fori_loop(0, NXS - 1, one, 0)
            two_a[q] = two_v[...]

        expect_by_core(
            stage + 1,
            (two_a.at[pl.ds(0, NXS // 2 - 1)], two_a),
            (one_a.at[pl.ds(0, NXS - 1)], None),
        )

    def corner_gram(one_a, two_a, stage):
        arrived(stage)
        arrived(stage + 1)
        ones = one_a[...].reshape(NXS // 2, 2, 8, 128)
        upper = two_a[...].reshape(128, 128)
        return jnp.concatenate(
            [
                jnp.concatenate([ones[:, 0].reshape(128, 128), upper], axis=1),
                jnp.concatenate([upper.T, ones[:, 1].reshape(128, 128)], axis=1),
            ],
            axis=0,
        )

    def send_src(piece_of, dst_ref, expected, stage):
        expect(stage, expected)

        def one(i, c):
            ss = plane_step(NXS - NSRC + i)[1]
            send(piece_of(ss), dst_ref, stage, at(z, x, ss))
            return c

        lax.fori_loop(0, NSRC - 1, one, 0)

    load_mic.wait()
    load_time.wait()
    mic = mic_ref[...]
    g1_v[...] = exact_dot(mic, mic, ((0,), (0,)))
    times = time_ref[...]
    gt_v[...] = exact_dot(times, times, ((0,), (0,)))
    mic_low = mic.astype(BF16).astype(F32)

    def make_kr(k, c):
        kr_v[pl.ds(pl.multiple_of(k * MIC_DEV, MIC_DEV), MIC_DEV), :] = (
            time_ref[pl.ds(k, 1), :] * mic_low
        ).astype(BF16)
        return c

    lax.fori_loop(0, SAMPLES, make_kr, 0)

    load_blk.wait()
    load.wait()
    for xx in range(NX):
        left = jnp.concatenate(
            [x_v[k, xx * 128 : (xx + 1) * 128, :] for k in range(SAMPLES)], axis=1
        )
        part = jnp.dot(left, kr_v[...], preferred_element_type=F32)
        for h in range(2):
            keep = blk_ref[0, xx * 2 + h].astype(F32)
            rows = slice(xx * 128 + h * 64, xx * 128 + (h + 1) * 64)
            y_v[rows, :] = part[h * 64 : (h + 1) * 64, :] * keep

    pl.semaphore_wait(barrier, NZ - 1 + NXS - 1)
    yield waiting

    send_x(g1_v, g1x_v, 0)

    for g in range(4):
        expect(3 + g, yx_v.at[0, pl.ds(0, 96), :])

        def row_group(ix, c, g=g):
            dx = ring_step(ix, NX)
            xx = (x + dx) % NX

            def one(i, c):
                zz = (z + ring_step(i)) % NZ
                send(
                    y_v.at[eight(xx * NZ + zz), :],
                    yx_v.at[dx - 1, eight(zz), :],
                    3 + g,
                    at(z, xx, src),
                )
                return c

            return lax.fori_loop(4 * g, 4 * g + 4, one, c)

        lax.fori_loop(0, NX - 1, row_group, 0)

    arrived(0)
    g1s_v[...] = (g1x_v[0] + g1x_v[1]) + (g1x_v[2] + g1x_v[3])
    corner_z(g1s_v, c1_v, d1_v, c1z_v, d1z_v, 23)

    expect(7, yz_v.at[pl.ds(0, NZ - 1)])
    for g in range(4):
        arrived(3 + g)

        def sum_send(i, c):
            zz = (z + ring_step(i)) % NZ
            rows = eight(zz)
            y128_v[rows, :] = (y_v[eight(x * NZ + zz), :] + yx_v[0, rows, :]) + (
                yx_v[1, rows, :] + yx_v[2, rows, :]
            )
            send(y128_v.at[rows, :], yz_v.at[i], 7, at(zz, x, src))
            return c

        lax.fori_loop(4 * g, min(4 * g + 4, NZ - 1), sum_send, 0)
    own = eight(z)
    yz_v[NZ - 1] = (y_v[eight(x * NZ + z), :] + yx_v[0, own, :]) + (
        yx_v[1, own, :] + yx_v[2, own, :]
    )
    yield waiting


    corner_sum(c1s_v, d1s_v, c1z_v, d1z_v, 23)
    corner_xs(c1s_v, d1s_v, c1a_v, d1a_v, 1)

    arrived(7)
    mine = eight(x * NZ + z)
    yall_v[mine, :] = jnp.sum(yz_v[...], axis=0)
    for g in range(4):
        last = min(4 * g + 4, NZ - 1)
        expect(8 + g, yall_v.at[pl.ds(0, 8 * (last - 4 * g)), :])

        def back_z(i, c, g=g):
            zz = (z + ring_step(i)) % NZ
            send(yall_v.at[mine, :], yall_v.at[mine, :], 8 + g, at(zz, x, src))
            return c

        lax.fori_loop(4 * g, last, back_z, 0)

    expect(12, yall_v.at[pl.ds(0, 128 * (NX - 1)), :])

    def forward(rows):
        def one(ix, c):
            xx = (x + ring_step(ix, NX)) % NX
            send(yall_v.at[rows, :], yall_v.at[rows, :], 12, at(z, xx, src))
            return c

        lax.fori_loop(0, NX - 1, one, 0)

    def forward_group(g):
        arrived(8 + g)

        def one(i, c):
            forward(eight(x * NZ + (z + NZ - ring_step(i)) % NZ))
            return c

        lax.fori_loop(4 * g, min(4 * g + 4, NZ - 1), one, 0)

    forward(mine)
    yield waiting

    def flip(k, c):
        xt_v[k] = x_v[k].T
        return c

    lax.fori_loop(0, SAMPLES, flip, 0)

    forward_group(3)
    forward_group(2)
    gram_mic = corner_gram(c1a_v, d1a_v, 1)
    yield waiting
    a_v[...] = gram_mic * gt_v[...] * (1.0 / (MIC_ALL * SAMPLES))
    invert(a_v, {1: lambda: forward_group(1), 3: lambda: forward_group(0)})
    yield waiting
    arrived(12)
    yield waiting
    raw = -exact_dot(yall_v[...], a_v[...])
    raw_v[...] = raw

    half = x // 2
    half_lanes = pl.ds(pl.multiple_of(half * 128, 128), 128)
    g2_v[...] = exact_dot(raw_v[:, half_lanes], raw, ((0,), (0,)))
    send_src(
        lambda ss: g2_v.at[eight((x % 2) * NSRC + ss), :],
        g2s_v.at[src],
        g2s_v.at[pl.ds(0, NSRC - 1)],
        13,
    )
    g2s_v[src] = g2_v[eight((x % 2) * NSRC + src), :]

    for b in range(SRC_DEV // SRC_BLK):
        keep = blk_ref[0, b].astype(F32)
        rows = slice(b * SRC_BLK, (b + 1) * SRC_BLK)
        low_v[rows, :] = (raw_v[rows, :] * keep).astype(BF16)

    def mic_part(kk, acc):
        left = xt_v[pl.ds(kk * 8, 8)].reshape(8 * MIC_DEV, SRC_DEV)
        prod = jnp.dot(left, low_v[...], preferred_element_type=F32)
        for i in range(8):
            piece = prod[i * MIC_DEV : (i + 1) * MIC_DEV, :]
            p_v[kk * 8 + i] = piece
            acc = acc + time_ref[pl.ds(kk * 8 + i, 1), :] * piece
        return acc

    mm_v[...] = lax.fori_loop(0, SAMPLES // 8, mic_part, jnp.zeros((MIC_DEV, RANK), F32))

    def sixteen(k):
        return pl.ds(pl.multiple_of(k * 16, 16), 16)

    mic_rows = sixteen(src)
    send_src(
        lambda ss: mm_v.at[sixteen(ss), :], mr_v.at[src], mr_v.at[pl.ds(0, NSRC - 1)], 15
    )
    mr_v[src] = mm_v[mic_rows, :]
    yield waiting
    arrived(13)
    g2p_v[...] = jnp.sum(g2s_v[...], axis=0)
    send_xs(g2p_v, g2a_v, 14)
    arrived(15)
    m16_v[...] = jnp.sum(mr_v[...], axis=0)
    send_xs(m16_v, mall_v, 16)
    arrived(14)
    yield waiting
    gram_src = g2a_v[...].reshape(RANK, RANK)
    src_row, src_col = scales_of(gram_src, SRC_ALL)
    gram_src = gram_src / (src_row * src_col)
    gn_v[...] = gram_src
    a_v[...] = gram_src * gt_v[...] * (1.0 / (SRC_ALL * SAMPLES))
    invert(a_v)
    yield waiting
    arrived(16)
    mraw = -exact_dot(mall_v[...].reshape(NX * MIC_DEV, RANK) / src_row, a_v[...])
    mraw_v[...] = mraw

    g3_v[...] = exact_dot(mraw_v[:, core_lanes], mraw, ((0,), (0,)))
    g3s_v[...] = g3_v[eight(q), :]
    corner_z(g3s_v, c3_v, d3_v, c3z_v, d3z_v, 25)

    mic_own = pl.ds(pl.multiple_of(x * MIC_DEV, MIC_DEV), MIC_DEV)

    def time_part(k, c):
        t_v[k] = jnp.sum(p_v[k] * mraw_v[mic_own, :], axis=0, keepdims=True)
        return c

    lax.fori_loop(0, SAMPLES, time_part, 0)
    expect(20, ts_v.at[pl.ds(0, NXS - 1)])

    def send_sample(i, c):
        xx, ss = plane_step(i)
        send(t_v.at[xx * NSRC + ss], ts_v.at[p], 20, at(z, xx, ss))
        return c

    lax.fori_loop(0, NXS - 1, send_sample, 0)
    ts_v[p] = t_v[p]
    yield waiting

    raw_v[...] = raw_v[...] / src_row
    store_src = pltpu.make_async_copy(raw_v, src_out, load_sem.at[0])
    store_src.start()
    arrived(20)
    tp_v[...] = jnp.sum(ts_v[...], axis=0)
    send_z(tp_v, tz_v, 21)
    corner_sum(c3s_v, d3s_v, c3z_v, d3z_v, 25)
    yield waiting
    corner_xs(c3s_v, d3s_v, c3a_v, d3a_v, 18)
    gram_mic = corner_gram(c3a_v, d3a_v, 18)
    yield waiting

    mic_row, mic_col = scales_of(gram_mic, MIC_ALL)
    a_v[...] = gn_v[...] * (gram_mic / (mic_row * mic_col)) * (1.0 / (SRC_ALL * MIC_ALL))
    store_mic = pltpu.make_async_copy(mraw_v.at[mic_own, :], mic_out, load_sem.at[1])

    def pass_on_time():
        arrived(21)
        tq_v[...] = jnp.sum(tz_v[...], axis=0)
        send_xs(tq_v, ta_v, 22)
        mraw_v[mic_own, :] = mraw_v[mic_own, :] / mic_row
        store_mic.start()

    factor(a_v, zf_v, wf_v, pass_on_time)
    yield waiting

    arrived(22)
    total = ta_v[...].reshape(SAMPLES, RANK)
    total = total / (src_row * mic_row)
    time_raw = exact_dot(exact_dot(total, zf_v[...], ((1,), (1,))), wf_v[...])
    time_diag = jnp.sum(time_raw * time_raw, axis=0, keepdims=True)
    time_v[...] = time_raw / jnp.sqrt(time_diag / SAMPLES + 1e-06)
    store_time = pltpu.make_async_copy(time_v, time_out, load_sem.at[2])
    store_time.start()
    store_src.wait()
    store_mic.wait()
    store_time.wait()

    yield waiting


def kernel(*refs, stop=None):
    send_sem, recv_sem = refs[-2:]
    for count, waiting in enumerate(sweep(*refs)):
        if count == stop:
            break
    for stage, (receive, leave, coming) in waiting.items():
        if coming:
            receive(recv_sem.at[stage])
        leave(send_sem.at[stage])


def copy_out(src_in, mic_in, time_in, src_out, mic_out, time_out):
    src_out[...] = src_in[...]
    mic_out[...] = mic_in[...]
    time_out[...] = time_in[...]


def on_device(tensor_slab, observed_blocks, mic_factor, time_factor, stop=None, collective_id=0, name=None):
    hbm = pl.BlockSpec(memory_space=pltpu.HBM)
    outs = (
        jax.ShapeDtypeStruct((SRC_DEV, RANK), F32),
        jax.ShapeDtypeStruct((MIC_DEV, RANK), F32),
        jax.ShapeDtypeStruct((SAMPLES, RANK), F32),
    )
    results = pl.pallas_call(
        functools.partial(kernel, stop=stop),
        name=name,
        out_shape=outs,
        in_specs=[hbm] * 4,
        out_specs=(hbm,) * 3,
        scratch_shapes=[
            pltpu.SMEM((1, SRC_DEV // SRC_BLK), jnp.int32),
            pltpu.VMEM((MIC_DEV, RANK), F32),
            pltpu.VMEM((SAMPLES, RANK), F32),
            pltpu.VMEM((SAMPLES, SRC_DEV, MIC_DEV), BF16),
            pltpu.VMEM((SAMPLES, MIC_DEV, SRC_DEV), BF16),
            pltpu.VMEM((SAMPLES * MIC_DEV, RANK), BF16),
            pltpu.VMEM((SAMPLES, MIC_DEV, RANK), F32),
            pltpu.VMEM((SRC_DEV, RANK), F32),
            pltpu.VMEM((NX - 1, 128, RANK), F32),
            pltpu.VMEM((128, RANK), F32),
            pltpu.VMEM((NZ, 8, RANK), F32),
            pltpu.VMEM((SRC_DEV, RANK), F32),
            pltpu.VMEM((SRC_DEV, RANK), F32),
            pltpu.VMEM((SRC_DEV, RANK), BF16),
            pltpu.VMEM((RANK, RANK), F32),
            pltpu.VMEM((RANK, RANK), F32),
            pltpu.VMEM((RANK, RANK), F32),
            pltpu.VMEM((RANK, RANK), F32),
            pltpu.VMEM((RANK, RANK), F32),
            pltpu.VMEM((RANK, RANK), F32),
            pltpu.VMEM((NX, 8, RANK), F32),
            pltpu.VMEM((8, RANK), F32),
            pltpu.VMEM((8, 128), F32),
            pltpu.VMEM((8, 128), F32),
            pltpu.VMEM((NZ, 8, 128), F32),
            pltpu.VMEM((NZ, 8, 128), F32),
            pltpu.VMEM((8, 128), F32),
            pltpu.VMEM((8, 128), F32),
            pltpu.VMEM((NXS, 8, 128), F32),
            pltpu.VMEM((NXS // 2, 8, 128), F32),
            pltpu.VMEM((128, RANK), F32),
            pltpu.VMEM((NSRC, 8, RANK), F32),
            pltpu.VMEM((8, RANK), F32),
            pltpu.VMEM((NXS, 8, RANK), F32),
            pltpu.VMEM((MIC_DEV, RANK), F32),
            pltpu.VMEM((NSRC, 16, RANK), F32),
            pltpu.VMEM((16, RANK), F32),
            pltpu.VMEM((NXS, 16, RANK), F32),
            pltpu.VMEM((NX * MIC_DEV, RANK), F32),
            pltpu.VMEM((128, RANK), F32),
            pltpu.VMEM((8, RANK), F32),
            pltpu.VMEM((8, 128), F32),
            pltpu.VMEM((8, 128), F32),
            pltpu.VMEM((NZ, 8, 128), F32),
            pltpu.VMEM((NZ, 8, 128), F32),
            pltpu.VMEM((8, 128), F32),
            pltpu.VMEM((8, 128), F32),
            pltpu.VMEM((NXS, 8, 128), F32),
            pltpu.VMEM((NXS // 2, 8, 128), F32),
            pltpu.VMEM((NXS, 1, RANK), F32),
            pltpu.VMEM((NXS, 1, RANK), F32),
            pltpu.VMEM((1, RANK), F32),
            pltpu.VMEM((NZ, 1, RANK), F32),
            pltpu.VMEM((1, RANK), F32),
            pltpu.VMEM((NXS, 1, RANK), F32),
            pltpu.VMEM((SAMPLES, RANK), F32),
            pltpu.SemaphoreType.DMA((4,)),
            pltpu.SemaphoreType.DMA((STAGES,)),
            pltpu.SemaphoreType.DMA((STAGES,)),
        ],
        compiler_params=pltpu.CompilerParams(
            collective_id=collective_id, has_side_effects=True, vmem_limit_bytes=60 * 1024 * 1024
        ),
    )(tensor_slab, observed_blocks.reshape(1, SRC_DEV // SRC_BLK), mic_factor, time_factor)
    vmem = pl.BlockSpec(memory_space=pltpu.VMEM)
    return pl.pallas_call(
        copy_out,
        out_shape=outs,
        in_specs=[vmem] * 3,
        out_specs=(vmem,) * 3,
        compiler_params=pltpu.CompilerParams(vmem_limit_bytes=60 * 1024 * 1024),
    )(*results)


def solution(mesh):
    placed = (P(None, "src", "mic"), P("src", "mic"), P("mic", None), P())
    return jax.shard_map(
        on_device,
        mesh=mesh,
        in_specs=placed,
        out_specs=(P("src", None), P("mic", None), P()),
        check_vma=False,
    )
```
